128 devices in a mesh: gx: 32 (over y, x, core), gy: 4 (over z).
Axes of the slice: x: 4, y: 4, z: 4, core: 2. Of those that a mesh axis runs over, the one named last changes fastest.
Arguments:
- adjoint_source: float32 [4, 256, 256, 512], P(None, 'gx', 'gy'), may hold values from -40 to 40, as said below
- conductivity: float32 [256, 256, 512], P('gx', 'gy'), may hold values from 0.1 to 10
- electrodes: int32 [4], replicated, may hold values from 0 to 65535
Outputs:
- solution_field: float32 [4, 256, 256, 512], P(None, 'gx', 'gy')
- residual: float32 [4, 256, 256, 512], P(None, 'gx', 'gy')
The draws below stay inside these ranges and needn't reach their ends.
Inputs may be any that keep to these rules, and one draw needn't show every extreme that they name: `electrodes`: each entry is a surface cell index, its first coordinate times 256 plus its second. `adjoint_source`: drawn afresh cell by cell.
All inputs are finite; a program needn't handle non-finite values.
Results may differ from the reference program's by a relative error of at most 0.0003.
Values sent between devices are 32-bit elements; how exact they have to be, the bound alone decides.
No kernel may reach another device: no remote copies, remote signals or barrier semaphores. Data moves between devices by JAX's collectives and lax.ppermute only.
A program may use at most 128 MiB of HBM per device.

```python
import math
import jax
import jax.numpy as jnp
from jax import lax

CZ = 512
SOURCES = 4
ITERS = 2
NX = 256
NY = 256


def draw_adjoint_source(key, part):
    key_base, key_column, key_cell = jax.random.split(key, 3)
    shape = (SOURCES, NX, NY, CZ)
    column_draw = jax.random.uniform(key_column, (SOURCES,), jnp.float32, 0.0, 1.0)
    column_level = (jnp.arange(SOURCES, dtype=jnp.float32) + column_draw) / SOURCES
    column = jnp.exp(column_level * math.log(10.0)).reshape(SOURCES, 1, 1, 1)
    cell = jnp.exp(jax.random.uniform(key_cell, (1, NX, NY, CZ), jnp.float32, 0.0, math.log(10.0)))
    position = jnp.arange(NX, dtype=jnp.float32) / max(NX - 1, 1)
    base = jax.random.truncated_normal(key_base, -6.0, 6.0, shape, jnp.float32)
    rise = jnp.exp(position * math.log(3.0))
    values = 0.1 * base * column * cell * rise[None, :, None, None]
    return jnp.clip(values, -40.0, 40.0)


def with_ends(values, rng, least, largest):
    dims = values.shape
    spot = [jax.random.randint(jax.random.fold_in(rng, axis), (), 0, dims[axis]) for axis in range(len(dims))]
    values = values.at[tuple(spot)].set(least)
    longest = dims.index(max(dims))
    spot[longest] = (spot[longest] + 1) % dims[longest]
    return values.at[tuple(spot)].set(largest)


def shard_levels(stream_key, dims, shards, least, high):
    gain = 1.0
    for dim, shards_of in shards:
        steps = jax.random.uniform(jax.random.fold_in(jax.random.fold_in(stream_key, 6), dim), (shards_of,), jnp.float32, least / len(shards), high / len(shards))
        gain = gain * jnp.repeat(jnp.exp(steps), dims[dim] // shards_of).reshape((-1,) + (1,) * (len(dims) - 1 - dim))
    return gain


def setup_inputs(seed: int = 0) -> dict:
    arg_keys = jax.random.split(jax.random.key(seed), 4)
    adjoint_source = draw_adjoint_source(jax.random.fold_in(arg_keys[3], 71), 0)
    conductivity = jnp.clip(jnp.exp(math.log(10.0) - 4.6051702 * jax.random.uniform(arg_keys[1], (NX, NY, CZ), jnp.float32) ** shard_levels(arg_keys[1], (NX, NY, CZ), ((0, 32), (1, 4)), -0.2, 0.2)), 0.1, 10.0)
    electrodes = with_ends(jax.random.randint(arg_keys[2], (SOURCES,), 0, NX * NY), jax.random.fold_in(arg_keys[2], 1), 0, (NX * NY) - 1).astype(jnp.int32)
    return dict(adjoint_source=adjoint_source, conductivity=conductivity, electrodes=electrodes)


def face_coefficients(padded):
    center = padded[1:-1, 1:-1, 1:-1]

    def face(neighbour):
        return jnp.where(neighbour > 0.0, 0.5 * (center + neighbour), center)
    return (face(padded[2:, 1:-1, 1:-1]), face(padded[:-2, 1:-1, 1:-1]), face(padded[1:-1, 2:, 1:-1]), face(padded[1:-1, :-2, 1:-1]), face(padded[1:-1, 1:-1, 2:]), face(padded[1:-1, 1:-1, :-2]))

def apply_operator(padded, coeffs):
    center = padded[:, 1:-1, 1:-1, 1:-1]
    others = (padded[:, 2:, 1:-1, 1:-1], padded[:, :-2, 1:-1, 1:-1], padded[:, 1:-1, 2:, 1:-1], padded[:, 1:-1, :-2, 1:-1], padded[:, 1:-1, 1:-1, 2:], padded[:, 1:-1, 1:-1, :-2])
    total = jnp.zeros(center.shape, jnp.float32)
    for coeff, other in zip(coeffs, others):
        total = total + coeff[None] * (center - other)
    return total

def gram(left, right):
    return jnp.einsum('ixyz,jxyz->ij', left, right, precision=lax.Precision.HIGHEST)

def combine(matrix, block):
    return jnp.einsum('ij,ixyz->jxyz', matrix, block, precision=lax.Precision.HIGHEST)

def small_solve(spd, rhs):
    factor = jnp.linalg.cholesky(spd)
    return jax.scipy.linalg.cho_solve((factor, True), rhs)

def reference(adjoint_source, conductivity, electrodes):
    coeffs = face_coefficients(jnp.pad(conductivity, 1))
    current = math.sqrt(NX * NY * CZ)
    row_x = (electrodes // NY).astype(jnp.int32)
    row_y = (electrodes % NY).astype(jnp.int32)
    mark_x = (jnp.arange(NX, dtype=jnp.int32)[None, :] == row_x[:, None]).astype(jnp.float32)
    mark_y = (jnp.arange(NY, dtype=jnp.int32)[None, :] == row_y[:, None]).astype(jnp.float32)
    spike = current * (mark_x[:, :, None] * mark_y[:, None, :])
    right_side = adjoint_source.at[:, :, :, 0].add(spike)
    solution_field = jnp.zeros_like(right_side)
    residual = right_side
    direction = right_side
    norm_now = gram(residual, residual)
    for step in range(ITERS):
        padded = jnp.pad(direction, ((0, 0), (1, 1), (1, 1), (1, 1)))
        image = apply_operator(padded, coeffs)
        curvature = gram(direction, image)
        alpha = small_solve(curvature, norm_now)
        solution_field = solution_field + combine(alpha, direction)
        residual = residual - combine(alpha, image)
        if step + 1 < ITERS:
            norm_next = gram(residual, residual)
            beta = small_solve(norm_now, norm_next)
            direction = residual + combine(beta, direction)
            norm_now = norm_next
    return (solution_field, residual)
```

```python
import functools
import math

import jax
import jax.numpy as jnp
from jax import lax
from jax.experimental import pallas as pl
from jax.experimental.pallas import tpu as pltpu
from jax.sharding import PartitionSpec as P

AXES = ("gx", "gy")
F = 4
NX = 8
NY = 64
NZ = 512
CHUNKS = NY // 8
PAIRS = [(i, j) for i in range(F) for j in range(i, F)]
L1_ROWS = (F + 1) * NY
L2_ROWS = F * NY + 16
IN_ROWS = L1_ROWS + L2_ROWS
G_ROWS = (F + 1) * 8 + F * 8
VMEM_LIMIT = 16 * 1024 * 1024

VM = pl.BlockSpec(memory_space=pltpu.VMEM)
SM = pl.BlockSpec(memory_space=pltpu.SMEM)
HBM = pl.BlockSpec(memory_space=pltpu.HBM)


def f32(*shape):
    return pltpu.VMEM(shape, jnp.float32)


def params():
    return pltpu.CompilerParams(vmem_limit_bytes=VMEM_LIMIT)


def cost(us):
    return pl.CostEstimate(flops=int(us * 4e6), bytes_accessed=int(us * 3.0e6), transcendentals=0)


def iota(dim):
    return lax.broadcasted_iota(jnp.int32, (8, NZ), dim)


def roll_z(v, shift):
    return pltpu.roll(v, shift % NZ, 1)


def row_up(load, i, halo):
    if i < CHUNKS - 1:
        return load(8 * i + 1)
    return jnp.where(iota(0) == 7, halo(), pltpu.roll(load(8 * i), 7, 0))


def row_down(load, i, halo):
    if i > 0:
        return load(8 * i - 1)
    return jnp.where(iota(0) == 0, halo(), pltpu.roll(load(8 * i), 1, 0))


def inside(h_other, h):
    return jnp.where(h_other > 0.0, h_other, h)


def z_coeffs(h):
    lane = iota(1)
    up = h + roll_z(h, -1)
    up_n = jnp.where(lane == NZ - 1, 0.0, up)
    down_n = roll_z(up_n, 1)
    total = jnp.where(lane == NZ - 1, 2.0 * h, up) + jnp.where(lane == 0, 2.0 * h, down_n)
    return up_n, down_n, total


def select_rows(ypar, r0, r1, start, count):
    a = r0[pl.ds(start, count), :]
    b = r1[pl.ds(start, count), :]
    return jnp.where(ypar == 0, b, a), jnp.where(ypar == 0, a, b)


def lanes_sum(p):
    return p[:, 0:128] + p[:, 128:256] + p[:, 256:384] + p[:, 384:512]


def add_gram(acc, base, left, right):
    for n, (i, j) in enumerate(PAIRS):
        acc[base + n] += lanes_sum(left[i] * right[j])


def add_spike(ref, index, row, current):
    tile = ref[(*index, slice(0, 128))]
    sub = lax.broadcasted_iota(jnp.int32, (8, 128), 0)
    lane = lax.broadcasted_iota(jnp.int32, (8, 128), 1)
    ref[(*index, slice(0, 128))] = tile + jnp.where((sub == row) & (lane == 0), current, 0.0)


def local_cell(elec, f):
    total_y = NY * lax.axis_size("gy")
    cell = elec[f]
    lx = cell // total_y - lax.axis_index("gx") * NX
    ly = cell % total_y - lax.axis_index("gy") * NY
    return lx, ly, (lx >= 0) & (lx < NX) & (ly >= 0) & (ly < NY)


def pack_kernel(current, adj, sigma, elec_in, l1_out, g0_out, g1_out, tiles, rows, elec, sems, esem):
    par = lax.axis_index("gx") % 2
    ypar = lax.axis_index("gy") % 2
    edge = par * (NX - 1)
    ecopy = pltpu.make_async_copy(elec_in, elec, esem)
    ecopy.start()
    copies = []
    for f in range(F + 1):
        src = adj.at[f] if f < F else sigma
        copies.append(
            pltpu.make_async_copy(src.at[edge], l1_out.at[pl.ds(f * NY, NY)], sems.at[0, f])
        )
        for side, y in ((0, 0), (1, NY - 8)):
            copies.append(
                pltpu.make_async_copy(
                    src.at[:, pl.ds(y, 8), :], tiles.at[f, side], sems.at[1 + side, f]
                )
            )
    for c in copies:
        c.start()
    ecopy.wait()
    for c in copies:
        c.wait()
    for f in range(F):
        lx, ly, here = local_cell(elec, f)

        @pl.when(here & (lx == edge))
        def _(f=f, ly=ly):
            r8 = pl.multiple_of((ly // 8) * 8, 8)
            add_spike(l1_out, (pl.ds(f * NY + r8, 8),), ly - r8, current)

        @pl.when(here & (ly < 8))
        def _(f=f, lx=lx, ly=ly):
            add_spike(tiles, (f, 0, lx, slice(0, 8)), ly, current)

        @pl.when(here & (ly >= NY - 8))
        def _(f=f, lx=lx, ly=ly):
            add_spike(tiles, (f, 1, lx, slice(0, 8)), ly - (NY - 8), current)

    h_rows = slice(F * NY, (F + 1) * NY)
    l1_out[h_rows, :] = 0.5 * l1_out[h_rows, :]
    for side, at in enumerate(((0, 1), (7, 6))):
        for depth, y in enumerate(at):
            for x in range(NX):
                for f in range(F + 1):
                    rows[side, depth, f * 8 + x : f * 8 + x + 1, :] = tiles[f, side, x, y : y + 1, :]
    h8 = slice(F * 8, F * 8 + 8)
    c_lo = 0.5 * (rows[0, 0, h8, :] + rows[0, 1, h8, :])
    c_hi = 0.5 * (rows[1, 0, h8, :] + rows[1, 1, h8, :])
    for f in range(F + 1):
        s = slice(f * 8, f * 8 + 8)
        k = 1.0 if f < F else 0.5
        lo, hi = k * rows[0, 0, s, :], k * rows[1, 0, s, :]
        g0_out[s, :] = jnp.where(ypar == 0, hi, lo)
        g1_out[s, :] = jnp.where(ypar == 0, lo, hi)
    for f in range(F):
        s = slice(f * 8, f * 8 + 8)
        lo = c_lo * (rows[0, 0, s, :] - rows[0, 1, s, :])
        hi = c_hi * (rows[1, 0, s, :] - rows[1, 1, s, :])
        d = slice((F + 1 + f) * 8, (F + 1 + f) * 8 + 8)
        g0_out[d, :] = jnp.where(ypar == 0, hi, lo)
        g1_out[d, :] = jnp.where(ypar == 0, lo, hi)


def pack(current, adj, sigma, electrodes):
    return pl.pallas_call(
        functools.partial(pack_kernel, current),
        out_shape=(f32(L1_ROWS, NZ), f32(G_ROWS, NZ), f32(G_ROWS, NZ)),
        in_specs=[HBM, HBM, HBM],
        out_specs=(VM,) * 3,
        scratch_shapes=[
            pltpu.VMEM((F + 1, 2, NX, 8, NZ), jnp.float32),
            pltpu.VMEM((2, 2, (F + 1) * 8, NZ), jnp.float32),
            pltpu.SMEM((F,), jnp.int32),
            pltpu.SemaphoreType.DMA((3, F + 1)),
            pltpu.SemaphoreType.DMA,
        ],
        compiler_params=params(),
        cost_estimate=cost(2),
        name="pack",
    )(adj, sigma, electrodes)


def load_kernel(current, adj, sigma, elec_in, b_out, h_out, acc, elec, sems, esem):
    ecopy = pltpu.make_async_copy(elec_in, elec, esem)
    ecopy.start()
    copies = [pltpu.make_async_copy(adj.at[f], b_out.at[f], sems.at[f]) for f in range(F)]
    copies.append(pltpu.make_async_copy(sigma, h_out, sems.at[F]))
    for c in copies:
        c.start()
    ecopy.wait()
    acc[...] = jnp.zeros(acc.shape, jnp.float32)
    for c in copies:
        c.wait()
    for f in range(F):
        lx, ly, here = local_cell(elec, f)

        @pl.when(here)
        def _(f=f, lx=lx, ly=ly):
            r8 = pl.multiple_of((ly // 8) * 8, 8)
            add_spike(b_out, (f, lx, pl.ds(r8, 8)), ly - r8, current)

    def plane(x, carry):
        for i in range(CHUNKS):
            r = slice(8 * i, 8 * i + 8)
            h_out[x, r, :] = 0.5 * h_out[x, r, :]
            vs = [b_out[f, x, r, :] for f in range(F)]
            add_gram(acc, 0, vs, vs)
        return carry

    lax.fori_loop(0, NX, plane, 0)


def load_fields(current, adj, sigma, electrodes):
    return pl.pallas_call(
        functools.partial(load_kernel, current),
        out_shape=(f32(F, NX, NY, NZ), f32(NX, NY, NZ), f32(10, 8, 128)),
        in_specs=[HBM, HBM, HBM],
        out_specs=(VM,) * 3,
        scratch_shapes=[
            pltpu.SMEM((F,), jnp.int32),
            pltpu.SemaphoreType.DMA((F + 1,)),
            pltpu.SemaphoreType.DMA,
        ],
        compiler_params=params(),
        cost_estimate=cost(3),
        name="load",
    )(adj, sigma, electrodes)


def chunk_coeffs(h_at, i, h_lo, h_hi, h_low=None, h_high=None):
    h = h_at(8 * i)
    up = h + row_up(h_at, i, lambda: inside(h_hi, h))
    down = h + row_down(h_at, i, lambda: inside(h_lo, h))
    zu, zd, total = z_coeffs(h)
    total = total + up + down
    xs = []
    for beside in (h_low, h_high):
        if beside is not None:
            xs.append(h + beside(8 * i))
            total = total + xs[-1]
        else:
            xs.append(None)
    return total, up, down, zu, zd, *xs


def chunk_apply(coeffs, load, low, high, i, lo_row, hi_row):
    total, up, down, zu, zd, xl, xh = coeffs
    v = load(8 * i)
    out = total * v - up * row_up(load, i, lambda: hi_row) - down * row_down(load, i, lambda: lo_row)
    out = out - zu * roll_z(v, -1) - zd * roll_z(v, 1)
    if xl is not None:
        out = out - xl * low(8 * i)
    if xh is not None:
        out = out - xh * high(8 * i)
    return v, out


def rows_of(ref, *index):
    return lambda r: ref[(*index, slice(r, r + 8), slice(None))]


def edge_kernel(b, h, r0, r1, y_out, l2_out, in_out):
    par = lax.axis_index("gx") % 2
    ypar = lax.axis_index("gy") % 2
    for n, x in enumerate((0, NX - 1)):
        beside = 1 if n == 0 else NX - 2
        h_lo, h_hi = select_rows(ypar, r0, r1, F * 8 + x, 1)
        rows = [select_rows(ypar, r0, r1, f * 8 + x, 1) for f in range(F)]
        for i in range(CHUNKS):
            side = {"h_high" if n == 0 else "h_low": rows_of(h, beside)}
            coeffs = chunk_coeffs(rows_of(h, x), i, h_lo, h_hi, **side)
            for f in range(F):
                other = rows_of(b, f, beside)
                _, out = chunk_apply(coeffs, rows_of(b, f, x), other, other, i, *rows[f])
                y_out[f, n, 8 * i : 8 * i + 8, :] = out
    far = par * (NX - 1)
    near = (NX - 1) - far
    in_out[F * NY : L1_ROWS, :] = h[near]
    for f in range(F):
        l2_out[f * NY : (f + 1) * NY, :] = y_out[f, par]
        in_out[f * NY : (f + 1) * NY, :] = b[f, near]
        in_out[L1_ROWS + f * NY : L1_ROWS + (f + 1) * NY, :] = y_out[f, 1 - par]
    l2_out[F * NY : L2_ROWS, :] = jnp.zeros((16, NZ), jnp.float32)
    in_out[L1_ROWS + F * NY : IN_ROWS, :] = jnp.zeros((16, NZ), jnp.float32)
    for f in range(F + 1):
        lo, hi = select_rows(ypar, r0, r1, f * 8 + far, 1)
        l2_out[F * NY + f : F * NY + f + 1, :] = lo
        l2_out[F * NY + 8 + f : F * NY + 8 + f + 1, :] = hi
        lo, hi = select_rows(ypar, r0, r1, f * 8 + near, 1)
        base = L1_ROWS + F * NY + f
        in_out[base : base + 1, :] = lo
        in_out[base + 8 : base + 9, :] = hi


def edge(b, h, r0, r1):
    return pl.pallas_call(
        edge_kernel,
        out_shape=(f32(F, 2, NY, NZ), f32(L2_ROWS, NZ), f32(IN_ROWS, NZ)),
        in_specs=[VM] * 4,
        out_specs=(VM,) * 3,
        compiler_params=params(),
        cost_estimate=cost(3),
        name="edge",
    )(b, h, r0, r1)


def row_halo(b, h, rh, side):
    y = 0 if side == 0 else NY - 1
    sub = iota(0)
    h_r = rh(F)
    h_own = jnp.concatenate([h[x, y : y + 1, :] for x in range(NX)], axis=0)
    zu, zd, total = z_coeffs(h_r)
    across = h_r + h_own
    up = jnp.where(sub == NX - 1, 0.0, h_r + pltpu.roll(h_r, 7, 0))
    down = jnp.where(sub == 0, 0.0, h_r + pltpu.roll(h_r, 1, 0))
    total = total + across + up + down
    outs = []
    for f in range(F):
        v = rh(f)
        own = jnp.concatenate([b[f, x, y : y + 1, :] for x in range(NX)], axis=0)
        out = total * v + rh(F + 1 + f) - across * own
        out = out - up * pltpu.roll(v, 7, 0) - down * pltpu.roll(v, 1, 0)
        out = out - zu * roll_z(v, -1) - zd * roll_z(v, 1)
        outs.append(jnp.where(h_r > 0.0, out, 0.0))
    return outs


def z_plane(h3, y3, h_rows, y_rows, store, acc):
    h_low, h_at, h_high = h3
    for i in range(CHUNKS):
        coeffs = chunk_coeffs(h_at, i, *h_rows, h_low, h_high)
        vs, outs = [], []
        for f in range(F):
            low, load, high = y3(f)
            v, out = chunk_apply(coeffs, load, low, high, i, *y_rows[f])
            store(f, 8 * i, out)
            vs.append(v)
            outs.append(out)
        add_gram(acc, 20, vs, outs)


def halo_of(x, yrows, hrows):
    h_rows = (hrows[0, pl.ds(x, 1), :], hrows[1, pl.ds(x, 1), :])
    y_rows = [(yrows[0, f, pl.ds(x, 1), :], yrows[1, f, pl.ds(x, 1), :]) for f in range(F)]
    return h_rows, y_rows


def inner_kernel(b, h, r0, r1, y, z, acc, yrows, hrows):
    ypar = lax.axis_index("gy") % 2
    acc[...] = jnp.zeros(acc.shape, jnp.float32)
    for side in range(2):
        rh = lambda f: select_rows(ypar, r0, r1, f * 8, 8)[side]
        hrows[side] = rh(F)
        for f, out in enumerate(row_halo(b, h, rh, side)):
            yrows[side, f] = out

    def y_plane(x, carry):
        h_lo, h_hi = select_rows(ypar, r0, r1, F * 8 + x, 1)
        rows = [select_rows(ypar, r0, r1, f * 8 + x, 1) for f in range(F)]
        for i in range(CHUNKS):
            coeffs = chunk_coeffs(
                rows_of(h, x), i, h_lo, h_hi, rows_of(h, x - 1), rows_of(h, x + 1)
            )
            vs, outs = [], []
            for f in range(F):
                low, load, high = (rows_of(b, f, x + d) for d in (-1, 0, 1))
                v, out = chunk_apply(coeffs, load, low, high, i, *rows[f])
                y[f, x - 1, 8 * i : 8 * i + 8, :] = out
                vs.append(v)
                outs.append(out)
            add_gram(acc, 0, vs, outs)
            add_gram(acc, 10, outs, outs)
        return carry

    lax.fori_loop(1, NX - 1, y_plane, 0)

    def z_loop(x, carry):
        def store(f, r, out):
            z[f, x - 2, r : r + 8, :] = out

        z_plane(
            [rows_of(h, x + d) for d in (-1, 0, 1)],
            lambda f: [rows_of(y, f, x - 1 + d) for d in (-1, 0, 1)],
            *halo_of(x, yrows, hrows),
            store,
            acc,
        )
        return carry

    lax.fori_loop(2, NX - 2, z_loop, 0)


def inner(b, h, r0, r1):
    return pl.pallas_call(
        inner_kernel,
        out_shape=(
            f32(F, NX - 2, NY, NZ),
            f32(F, NX - 4, NY, NZ),
            f32(30, 8, 128),
            f32(2, F, 8, NZ),
            f32(2, 8, NZ),
        ),
        in_specs=[VM] * 4,
        out_specs=(VM,) * 5,
        compiler_params=params(),
        cost_estimate=cost(8),
        name="inner",
    )(b, h, r0, r1)


def outer_kernel(
    b, h, rl1, rl2, rin, r0, r1, ye, yi, accb, acc_in, yr_in, hrows,
    yo, zo, msg,
    acc, yhalo, hhalo, yrows,
):
    par = lax.axis_index("gx") % 2
    ypar = lax.axis_index("gy") % 2
    acc[...] = acc_in[...]
    yrows[...] = yr_in[...]
    for n, first, second, s0 in ((par, rl1, rl2, 0), (1 - par, rin, rin, L1_ROWS)):
        x = n * (NX - 1)
        for i in range(CHUNKS):
            r = 8 * i
            own = h[x, r : r + 8, :]
            there = first[F * NY + r : F * NY + r + 8, :]
            beyond = inside(there, own)
            hhalo[n, r : r + 8, :] = beyond
            c = own + beyond
            vs, outs = [], []
            for f in range(F):
                v = b[f, x, r : r + 8, :]
                flux = c * (v - first[f * NY + r : f * NY + r + 8, :])
                out = ye[f, n, r : r + 8, :] + flux
                yo[f, n, r : r + 8, :] = out
                other = second[s0 + f * NY + r : s0 + f * NY + r + 8, :] - flux
                yhalo[f, n, r : r + 8, :] = jnp.where(there > 0.0, other, 0.0)
                vs.append(v)
                outs.append(out)
            add_gram(acc, 0, vs, outs)
            add_gram(acc, 10, outs, outs)
        for side in range(2):
            base = s0 + F * NY + 8 * side
            h_r = hrows[side, pl.ds(x, 1), :]
            h_c = second[base + F : base + F + 1, :]
            c = h_r + inside(h_c, h_r)
            for f in range(F):
                v = select_rows(ypar, r0, r1, f * 8 + x, 1)[side]
                add = jnp.where(h_r > 0.0, c * (v - second[base + f : base + f + 1, :]), 0.0)
                yrows[side, f, pl.ds(x, 1), :] = yrows[side, f, pl.ds(x, 1), :] + add
    h_of = lambda x: rows_of(hhalo, 0 if x < 0 else 1) if x in (-1, NX) else rows_of(h, x)

    def y_of(f, x):
        if x in (-1, NX):
            return rows_of(yhalo, f, 0 if x < 0 else 1)
        if x in (0, NX - 1):
            return rows_of(yo, f, 0 if x == 0 else 1)
        return rows_of(yi, f, x - 1)

    for n, x in enumerate((0, 1, NX - 2, NX - 1)):

        def store(f, r, out, n=n):
            zo[f, n, r : r + 8, :] = out

        z_plane(
            [h_of(x + d) for d in (-1, 0, 1)],
            lambda f: [y_of(f, x + d) for d in (-1, 0, 1)],
            *halo_of(x, yrows, hrows),
            store,
            acc,
        )
    sums = jnp.concatenate(
        [jnp.sum(accb[k], axis=0, keepdims=True) for k in range(10)]
        + [jnp.sum(acc[k], axis=0, keepdims=True) for k in range(30)]
        + [jnp.zeros((88, 128), jnp.float32)],
        axis=0,
    )
    msg[...] = lax.dot_general(
        jnp.ones((8, 128), jnp.float32),
        sums,
        (((1,), (1,)), ((), ())),
        precision=lax.Precision.HIGHEST,
        preferred_element_type=jnp.float32,
    )


def outer(b, h, rl1, rl2, rin, r0, r1, ye, yi, accb, acc, yrows, hrows):
    return pl.pallas_call(
        outer_kernel,
        out_shape=(f32(F, 2, NY, NZ), f32(F, 4, NY, NZ), f32(8, 128)),
        in_specs=[VM] * 13,
        out_specs=(VM,) * 3,
        scratch_shapes=[
            pltpu.VMEM((30, 8, 128), jnp.float32),
            pltpu.VMEM((F, 2, NY, NZ), jnp.float32),
            pltpu.VMEM((2, NY, NZ), jnp.float32),
            pltpu.VMEM((2, F, 8, NZ), jnp.float32),
        ],
        compiler_params=params(),
        cost_estimate=cost(5),
        name="outer",
    )(b, h, rl1, rl2, rin, r0, r1, ye, yi, accb, acc, yrows, hrows)


def mm(a, b, ta=False):
    at = (lambda i, k: a[k][i]) if ta else (lambda i, k: a[i][k])
    return [
        [sum((at(i, k) * b[k][j] for k in range(1, F)), at(i, 0) * b[0][j]) for j in range(F)]
        for i in range(F)
    ]


def add(a, b, s=1.0):
    return [[a[i][j] + s * b[i][j] for j in range(F)] for i in range(F)]


def symmetric(a):
    return [[a[i][j] if i == j else 0.5 * (a[i][j] + a[j][i]) for j in range(F)] for i in range(F)]


def spd_solve(a, b):
    low = [[None] * F for _ in range(F)]
    d, inv = [None] * F, [None] * F
    for j in range(F):
        t = a[j][j]
        for k in range(j):
            t = t - low[j][k] * low[j][k] * d[k]
        d[j] = t
        inv[j] = 1.0 / t
        for i in range(j + 1, F):
            t = a[i][j]
            for k in range(j):
                t = t - low[i][k] * low[j][k] * d[k]
            low[i][j] = t * inv[j]
    x = [list(row) for row in b]
    for i in range(F):
        for k in range(i):
            for j in range(F):
                x[i][j] = x[i][j] - low[i][k] * x[k][j]
    for i in range(F):
        x[i] = [e * inv[i] for e in x[i]]
    for i in reversed(range(F)):
        for k in range(i + 1, F):
            for j in range(F):
                x[i][j] = x[i][j] - low[k][i] * x[k][j]
    return x


def step_matrices(entry):
    grams = []
    for g in range(4):
        m = [[None] * F for _ in range(F)]
        for n, (i, j) in enumerate(PAIRS):
            m[i][j] = m[j][i] = entry(10 * g + n)
        grams.append(m)
    bb, by, yy, yz = grams
    alpha = spd_solve(by, bb)
    new = symmetric(add(mm(alpha, mm(yy, alpha), ta=True), bb, -1.0))
    beta = spd_solve(bb, new)
    e = [[beta[i][j] + 1.0 if i == j else beta[i][j] for j in range(F)] for i in range(F)]
    cross = mm(e, mm(yy, alpha), ta=True)
    curv = add(mm(e, mm(by, e), ta=True), mm(alpha, mm(yz, alpha), ta=True))
    curv = [[curv[i][j] - cross[i][j] - cross[j][i] for j in range(F)] for i in range(F)]
    alpha2 = spd_solve(symmetric(curv), new)
    m1 = add(alpha, mm(e, alpha2))
    m2 = mm(alpha, alpha2)
    return m1, m2


def final_kernel(w, b, yo, yi, zo, zi, xs_out, res_out, coef):
    x = pl.program_id(0)

    @pl.when(x == 0)
    def _():
        total = jnp.sum(w[...], axis=0, keepdims=True)
        sub = lax.broadcasted_iota(jnp.int32, (128, 128), 0)
        lane = lax.broadcasted_iota(jnp.int32, (128, 128), 1)
        spread = lax.dot_general(
            jnp.where(sub == lane, total, 0.0),
            jnp.ones((128, 128), jnp.float32),
            (((1,), (0,)), ((), ())),
            precision=lax.Precision.HIGHEST,
            preferred_element_type=jnp.float32,
        )
        m1, m2 = step_matrices(lambda k: spread[k : k + 1, :])
        for i in range(F):
            for j in range(F):
                coef[i * F + j] = jnp.broadcast_to(m1[i][j], (8, 128))
                coef[16 + i * F + j] = jnp.broadcast_to(m2[i][j], (8, 128))

    def planes(y_at, z_at):
        def body(i, carry):
            r = pl.ds(pl.multiple_of(i * 8, 8), 8)
            for q in range(NZ // 128):
                s = slice(q * 128, q * 128 + 128)
                bs = [b[f, x, r, s] for f in range(F)]
                ys = [y_at[0][f, y_at[1], r, s] for f in range(F)]
                zs = [z_at[0][f, z_at[1], r, s] for f in range(F)]
                for j in range(F):
                    xo, ro = None, bs[j]
                    for k in range(F):
                        c1 = coef[k * F + j]
                        c2 = coef[16 + k * F + j]
                        t = bs[k] * c1 - ys[k] * c2
                        xo = t if xo is None else xo + t
                        ro = ro - ys[k] * c1 + zs[k] * c2
                    xs_out[j, 0, r, s] = xo
                    res_out[j, 0, r, s] = ro
            return carry

        lax.fori_loop(0, CHUNKS, body, 0)

    high = x >= NX // 2

    @pl.when((x == 0) | (x == NX - 1))
    def _():
        n = jnp.where(high, 1, 0)
        planes((yo, n), (zo, 3 * n))

    @pl.when((x == 1) | (x == NX - 2))
    def _():
        planes((yi, x - 1), (zo, jnp.where(high, 2, 1)))

    @pl.when((x > 1) & (x < NX - 2))
    def _():
        planes((yi, x - 1), (zi, x - 2))


def final(w, b, yo, yi, zo, zi):
    block = pl.BlockSpec((F, 1, NY, NZ), lambda x: (0, x, 0, 0))
    return pl.pallas_call(
        final_kernel,
        grid=(NX,),
        out_shape=(
            jax.ShapeDtypeStruct((F, NX, NY, NZ), jnp.float32),
            jax.ShapeDtypeStruct((F, NX, NY, NZ), jnp.float32),
        ),
        in_specs=[VM] * 6,
        out_specs=(block, block),
        scratch_shapes=[pltpu.VMEM((32, 8, 128), jnp.float32)],
        compiler_params=params(),
        cost_estimate=cost(5),
        name="final",
    )(w, b, yo, yi, zo, zi)


def exchange(x, sizes, partner):
    nx, ny = sizes
    pairs = []
    for a in range(nx):
        for c in range(ny):
            ta, tc = partner(a, c)
            if 0 <= ta < nx and 0 <= tc < ny:
                pairs.append((a * ny + c, ta * ny + tc))
    return lax.ppermute(x, AXES, pairs)


def shards(sizes, adjoint_source, conductivity, electrodes):
    nx, ny = sizes
    current = math.sqrt(nx * NX * ny * NY * NZ)
    l1, g0, g1 = pack(current, adjoint_source, conductivity, electrodes)
    rl1 = exchange(l1, sizes, lambda a, c: (a + 1 if a % 2 else a - 1, c))
    r0 = exchange(g0, sizes, lambda a, c: (a, c ^ 1))
    r1 = exchange(g1, sizes, lambda a, c: (a, c + 1 if c % 2 else c - 1))
    b, h, accb = load_fields(current, adjoint_source, conductivity, electrodes)
    ye, l2, intra = edge(b, h, r0, r1)
    rl2 = exchange(l2, sizes, lambda a, c: (a + 1 if a % 2 else a - 1, c))
    rin = exchange(intra, sizes, lambda a, c: (a ^ 1, c))
    yi, zi, acc, yrows, hrows = inner(b, h, r0, r1)
    yo, zo, msg = outer(b, h, rl1, rl2, rin, r0, r1, ye, yi, accb, acc, yrows, hrows)
    sent = jnp.broadcast_to(msg[0:1][None], (nx * ny, 1, 128))
    w = lax.all_to_all(sent, AXES, 0, 0).reshape(nx * ny, 128)
    return final(w, b, yo, yi, zo, zi)


def solution(mesh):
    sizes = (mesh.shape["gx"], mesh.shape["gy"])
    placed = (P(None, "gx", "gy", None), P("gx", "gy", None), P())
    return jax.shard_map(
        functools.partial(shards, sizes),
        mesh=mesh,
        in_specs=placed,
        out_specs=(P(None, "gx", "gy", None), P(None, "gx", "gy", None)),
        check_vma=False,
    )
```

```python
import functools
import math

import jax
import jax.numpy as jnp
from jax import lax
from jax.experimental import pallas as pl
from jax.experimental.pallas import tpu as pltpu
from jax.sharding import PartitionSpec as P

AXES = ("gx", "gy")
F = 4
NX = 8
NY = 64
NZ = 512
Q = NZ // 128
CHUNKS = NY // 8
UNROLL = 2
PAIRS = [(i, j) for i in range(F) for j in range(i, F)]
TOP = 8
ROWS = NY + 2 * TOP
PLANE = Q * NY
L1_ROWS = (F + 1) * PLANE
CORNER = 24
L2_ROWS = F * PLANE + 2 * CORNER
IN_ROWS = L1_ROWS + L2_ROWS
TILE_ROWS = (F + 1) * Q * 8
G_ROWS = TILE_ROWS + F * Q * 8
VMEM_LIMIT = 16 * 1024 * 1024

VM = pl.BlockSpec(memory_space=pltpu.VMEM)
HBM = pl.BlockSpec(memory_space=pltpu.HBM)


def f32(*shape):
    return pltpu.VMEM(shape, jnp.float32)


def params():
    return pltpu.CompilerParams(vmem_limit_bytes=VMEM_LIMIT)


def cost(us):
    return pl.CostEstimate(flops=int(us * 4e6), bytes_accessed=int(us * 3.0e6), transcendentals=0)


def in_hbm(*arrays):
    return tuple(pltpu.with_memory_space_constraint(a, pltpu.HBM) for a in arrays)


def iota(dim):
    return lax.broadcasted_iota(jnp.int32, (8, 128), dim)


def inside(h_other, h):
    return jnp.where(h_other > 0.0, h_other, h)


def above_z(v):
    t = [pltpu.roll(a, 127, 1) for a in v]
    last = iota(1) == 127
    return [jnp.where(last, t[q + 1], t[q]) if q < Q - 1 else t[q] for q in range(Q)]


def below_z(v):
    t = [pltpu.roll(a, 1, 1) for a in v]
    first = iota(1) == 0
    return [jnp.where(first, t[q - 1], t[q]) if q > 0 else t[q] for q in range(Q)]


def z_coeffs(h):
    up = [a + b for a, b in zip(h, above_z(h))]
    edge = iota(1) == 127
    total = up[:-1] + [jnp.where(edge, 2.0 * h[-1], up[-1])]
    up[-1] = jnp.where(edge, 0.0, up[-1])
    down = below_z(up)
    first = jnp.where(iota(1) == 0, 2.0 * h[0], down[0])
    total = [t + d for t, d in zip(total, [first] + down[1:])]
    down[0] = jnp.where(iota(1) == 0, 0.0, down[0])
    return up, down, total


def add_gram(acc, base, left, right):
    for n, (i, j) in enumerate(PAIRS):
        t = left[i][0] * right[j][0]
        for q in range(1, Q):
            t = t + left[i][q] * right[j][q]
        acc[base + n] += t


def chunk_loop(body):
    def step(i, carry):
        for u in range(UNROLL):
            body(pl.multiple_of(i * (8 * UNROLL), 8) + 8 * u)
        return carry

    lax.fori_loop(0, CHUNKS // UNROLL, step, 0)


def tiles_of(ref, index, row):
    return [ref[(*index, q, pl.ds(row, 8), slice(None))] for q in range(Q)]


def add_spike(ref, index, row, current):
    tile = ref[(*index, slice(0, 128))]
    ref[(*index, slice(0, 128))] = tile + jnp.where(
        (iota(0) == row) & (iota(1) == 0), current, 0.0
    )


def local_cell(elec, f):
    total_y = NY * lax.axis_size("gy")
    cell = elec[f]
    lx = cell // total_y - lax.axis_index("gx") * NX
    ly = cell % total_y - lax.axis_index("gy") * NY
    return lx, ly, (lx >= 0) & (lx < NX) & (ly >= 0) & (ly < NY)


def pack_kernel(
    current, adj, sigma, elec_in, l1_out, g0_out, g1_out, own_out, plane, tiles, far_rows, elec, sems, esem
):
    par = lax.axis_index("gx") % 2
    ypar = lax.axis_index("gy") % 2
    edge = par * (NX - 1)
    ecopy = pltpu.make_async_copy(elec_in, elec, esem)
    ecopy.start()
    copies = []
    for f in range(F + 1):
        src = adj.at[f] if f < F else sigma
        copies.append(pltpu.make_async_copy(src.at[edge], plane.at[f], sems.at[0, f]))
        for side, y in ((0, 0), (1, NY - 8)):
            copies.append(
                pltpu.make_async_copy(
                    src.at[:, pl.ds(y, 8), :], tiles.at[f, side], sems.at[1 + side, f]
                )
            )
    for c in copies:
        c.start()
    ecopy.wait()
    for c in copies:
        c.wait()
    for f in range(F):
        lx, ly, here = local_cell(elec, f)

        @pl.when(here & (lx == edge))
        def _(f=f, ly=ly):
            r8 = pl.multiple_of((ly // 8) * 8, 8)
            add_spike(plane, (f, pl.ds(r8, 8)), ly - r8, current)

        @pl.when(here & (ly < 8))
        def _(f=f, lx=lx, ly=ly):
            add_spike(tiles, (f, 0, lx, slice(0, 8)), ly, current)

        @pl.when(here & (ly >= NY - 8))
        def _(f=f, lx=lx, ly=ly):
            add_spike(tiles, (f, 1, lx, slice(0, 8)), ly - (NY - 8), current)

    for f in range(F + 1):
        k = 1.0 if f < F else 0.5
        for q in range(Q):
            s = slice(q * 128, q * 128 + 128)
            a = (f * Q + q) * NY
            l1_out[a : a + NY, :] = k * plane[f, :, s]
            for x in range(NX):
                a = (f * Q + q) * 8 + x
                for side, (near, far) in enumerate(((0, 1), (7, 6))):
                    own_out[side, a : a + 1, :] = k * tiles[f, side, x, near : near + 1, s]
                    far_rows[side, a : a + 1, :] = k * tiles[f, side, x, far : far + 1, s]
    for f in range(F + 1):
        for q in range(Q):
            t = slice((f * Q + q) * 8, (f * Q + q) * 8 + 8)
            lo, hi = own_out[0, t, :], own_out[1, t, :]
            g0_out[t, :] = jnp.where(ypar == 0, hi, lo)
            g1_out[t, :] = jnp.where(ypar == 0, lo, hi)
            if f < F:
                ht = slice((F * Q + q) * 8, (F * Q + q) * 8 + 8)
                lo = (own_out[0, ht, :] + far_rows[0, ht, :]) * (lo - far_rows[0, t, :])
                hi = (own_out[1, ht, :] + far_rows[1, ht, :]) * (hi - far_rows[1, t, :])
                d = slice(TILE_ROWS + (f * Q + q) * 8, TILE_ROWS + (f * Q + q) * 8 + 8)
                g0_out[d, :] = jnp.where(ypar == 0, hi, lo)
                g1_out[d, :] = jnp.where(ypar == 0, lo, hi)


def pack(current, adj, sigma, electrodes):
    return pl.pallas_call(
        functools.partial(pack_kernel, current),
        out_shape=(
            f32(L1_ROWS, 128),
            f32(G_ROWS, 128),
            f32(G_ROWS, 128),
            f32(2, TILE_ROWS, 128),
        ),
        in_specs=[HBM] * 3,
        out_specs=(VM,) * 4,
        scratch_shapes=[
            pltpu.VMEM((F + 1, NY, NZ), jnp.float32),
            pltpu.VMEM((F + 1, 2, NX, 8, NZ), jnp.float32),
            pltpu.VMEM((2, TILE_ROWS, 128), jnp.float32),
            pltpu.SMEM((F,), jnp.int32),
            pltpu.SemaphoreType.DMA((3, F + 1)),
            pltpu.SemaphoreType.DMA,
        ],
        compiler_params=params(),
        cost_estimate=cost(2),
        name="pack",
    )(*in_hbm(adj, sigma, electrodes))


def load_kernel(current, adj, sigma, elec_in, b_out, h_out, acc, fields, cond, elec, sems, esem):
    ecopy = pltpu.make_async_copy(elec_in, elec, esem)
    ecopy.start()
    copies = [pltpu.make_async_copy(adj.at[f], fields.at[f], sems.at[f]) for f in range(F)]
    copies.append(pltpu.make_async_copy(sigma, cond, sems.at[F]))
    for c in copies:
        c.start()
    ecopy.wait()
    acc[...] = jnp.zeros(acc.shape, jnp.float32)
    for c in copies:
        c.wait()
    for f in range(F):
        lx, ly, here = local_cell(elec, f)

        @pl.when(here)
        def _(f=f, lx=lx, ly=ly):
            r8 = pl.multiple_of((ly // 8) * 8, 8)
            add_spike(fields, (f, lx, pl.ds(r8, 8)), ly - r8, current)

    def plane(x, carry):
        def chunk(r):
            vs = []
            for f in range(F):
                v = [fields[f, x, pl.ds(r, 8), q * 128 : q * 128 + 128] for q in range(Q)]
                for q in range(Q):
                    b_out[f, x, q, pl.ds(r + TOP, 8), :] = v[q]
                vs.append(v)
            for q in range(Q):
                h_out[x + 1, q, pl.ds(r + TOP, 8), :] = (
                    0.5 * cond[x, pl.ds(r, 8), q * 128 : q * 128 + 128]
                )
            add_gram(acc, 0, vs, vs)

        chunk_loop(chunk)
        return carry

    lax.fori_loop(0, NX, plane, 0)


def load_fields(current, adj, sigma, electrodes):
    return pl.pallas_call(
        functools.partial(load_kernel, current),
        out_shape=(f32(F, NX, Q, ROWS, 128), f32(NX + 2, Q, ROWS, 128), f32(10, 8, 128)),
        in_specs=[HBM] * 3,
        out_specs=(VM,) * 3,
        scratch_shapes=[
            pltpu.VMEM((F, NX, NY, NZ), jnp.float32),
            pltpu.VMEM((NX, NY, NZ), jnp.float32),
            pltpu.SMEM((F,), jnp.int32),
            pltpu.SemaphoreType.DMA((F + 1,)),
            pltpu.SemaphoreType.DMA,
        ],
        compiler_params=params(),
        cost_estimate=cost(3),
        name="load",
    )(*in_hbm(adj, sigma, electrodes))


def chunk_coeffs(h, k, r, low=True, high=True):
    at = r + TOP
    own = tiles_of(h, (k,), at)
    up, down, total = z_coeffs(own)
    faces = [(None, up), (None, down)]
    others = [((0, 1), tiles_of(h, (k,), at + 1)), ((0, -1), tiles_of(h, (k,), at - 1))]
    if low:
        others.append(((-1, 0), tiles_of(h, (k - 1,), at)))
    if high:
        others.append(((1, 0), tiles_of(h, (k + 1,), at)))
    for step, other in others:
        c = [a + b for a, b in zip(own, other)]
        total = [a + b for a, b in zip(total, c)]
        faces.append((step, c))
    return total, faces


def chunk_apply(coeffs, v, f, k, r):
    total, faces = coeffs
    at = r + TOP
    own = tiles_of(v, (f, k), at)
    beside = [above_z(own), below_z(own)]
    beside += [tiles_of(v, (f, k + s[0]), at + s[1]) for s, _ in faces[2:]]
    out = []
    for q in range(Q):
        t = total[q] * own[q]
        for (_, c), n in zip(faces, beside):
            t = t - c[q] * n[q]
        out.append(t)
    return own, out


def side_planes(par):
    far = par * (NX - 1)
    near = (NX - 1) - far
    return far, near, par * (NX + 1), (1 - par) * (NX + 1)


def halo_select(ypar, r0, r1, item):
    a = r0[item * 8 : item * 8 + 8, :]
    b = r1[item * 8 : item * 8 + 8, :]
    return jnp.where(ypar == 0, b, a), jnp.where(ypar == 0, a, b)


def edge_kernel(b_in, h_in, own, r0, r1, rl1, b, h, y, l2_out, in_out, g):
    del b_in, h_in
    par = lax.axis_index("gx") % 2
    ypar = lax.axis_index("gy") % 2
    far, near, far_halo, _ = side_planes(par)
    for item in range((F + 1) * Q):
        f, q = divmod(item, Q)
        for side, t in enumerate(halo_select(ypar, r0, r1, item)):
            row = TOP - 1 if side == 0 else TOP + NY
            g[side, item * 8 : item * 8 + 8, :] = t
            if f < F:
                for x in range(NX):
                    b[f, x, q, row : row + 1, :] = g[side, item * 8 + x : item * 8 + x + 1, :]
            else:
                t = inside(t, own[side, item * 8 : item * 8 + 8, :])
                g[2 + side, q * 8 : q * 8 + 8, :] = t
                for x in range(NX):
                    h[x + 1, q, row : row + 1, :] = g[2 + side, q * 8 + x : q * 8 + x + 1, :]
    for x in (0, NX - 1):

        def chunk(r, x=x):
            coeffs = chunk_coeffs(h, x + 1, r, low=x > 0, high=x == 0)
            for f in range(F):
                _, out = chunk_apply(coeffs, b, f, x, r)
                for q in range(Q):
                    y[f, x + 1, q, pl.ds(r + TOP, 8), :] = out[q]

        chunk_loop(chunk)
    data = slice(TOP, TOP + NY)
    for q in range(Q):
        for f in range(F):
            a = (f * Q + q) * NY
            l2_out[a : a + NY, :] = y[f, far + 1, q, data, :]
            in_out[a : a + NY, :] = b[f, near, q, data, :]
            in_out[L1_ROWS + a : L1_ROWS + a + NY, :] = y[f, near + 1, q, data, :]
        a = (F * Q + q) * NY
        in_out[a : a + NY, :] = h[near + 1, q, data, :]
    base = F * PLANE
    l2_out[base:L2_ROWS, :] = jnp.zeros((2 * CORNER, 128), jnp.float32)
    in_out[L1_ROWS + base : IN_ROWS, :] = jnp.zeros((2 * CORNER, 128), jnp.float32)
    for side in range(2):
        for item in range((F + 1) * Q):
            a = base + side * CORNER + item
            l2_out[a : a + 1, :] = g[side, pl.ds(item * 8 + far, 1), :]
            in_out[L1_ROWS + a : L1_ROWS + a + 1, :] = g[side, pl.ds(item * 8 + near, 1), :]
    border(b, h, y, rl1, far, far_halo)


def border(b, h, y, first, x, halo):
    def chunk(r):
        for q in range(Q):
            own = h[x + 1, q, pl.ds(r + TOP, 8), :]
            beyond = inside(first[pl.ds((F * Q + q) * NY + r, 8), :], own)
            h[halo, q, pl.ds(r + TOP, 8), :] = beyond
            c = own + beyond
            for f in range(F):
                v = b[f, x, q, pl.ds(r + TOP, 8), :]
                flux = c * (v - first[pl.ds((f * Q + q) * NY + r, 8), :])
                at = (f, x + 1, q, pl.ds(r + TOP, 8), slice(None))
                y[at] = y[at] + flux

    chunk_loop(chunk)


def edge(b, h, own, r0, r1, rl1):
    return pl.pallas_call(
        edge_kernel,
        out_shape=(
            f32(F, NX, Q, ROWS, 128),
            f32(NX + 2, Q, ROWS, 128),
            f32(F, NX + 2, Q, ROWS, 128),
            f32(L2_ROWS, 128),
            f32(IN_ROWS, 128),
        ),
        in_specs=[VM] * 6,
        out_specs=(VM,) * 5,
        input_output_aliases={0: 0, 1: 1},
        scratch_shapes=[pltpu.VMEM((4, TILE_ROWS, 128), jnp.float32)],
        compiler_params=params(),
        cost_estimate=cost(10),
        name="edge",
    )(b, h, own, r0, r1, rl1)


def row_halo(own, rh, side, y, tmp):
    count = lax.axis_size("gy")
    ay = lax.axis_index("gy")
    valid = ay > 0 if side == 0 else ay < count - 1
    row = TOP - 1 if side == 0 else TOP + NY
    sub = iota(0)
    own_at = lambda f, q: own[side, (f * Q + q) * 8 : (f * Q + q) * 8 + 8, :]
    h_r = [rh(F * Q + q) for q in range(Q)]
    zu, zd, total = z_coeffs(h_r)
    across = [h_r[q] + own_at(F, q) for q in range(Q)]
    up = [jnp.where(sub == NX - 1, 0.0, a + pltpu.roll(a, 7, 0)) for a in h_r]
    down = [jnp.where(sub == 0, 0.0, a + pltpu.roll(a, 1, 0)) for a in h_r]
    total = [sum(t) for t in zip(total, across, up, down)]
    for f in range(F):
        v = [rh(f * Q + q) for q in range(Q)]
        zp, zm = above_z(v), below_z(v)
        for q in range(Q):
            out = total[q] * v[q] + rh((F + 1 + f) * Q + q) - across[q] * own_at(f, q)
            out = out - up[q] * pltpu.roll(v[q], 7, 0) - down[q] * pltpu.roll(v[q], 1, 0)
            out = out - zu[q] * zp[q] - zd[q] * zm[q]
            tmp[side, f, q] = jnp.where(valid, out, 0.0)
            for x in range(NX):
                y[f, x + 1, q, row : row + 1, :] = tmp[side, f, q, x : x + 1, :]


def z_plane(h, y, z, acc, x):
    def chunk(r):
        coeffs = chunk_coeffs(h, x + 1, r)
        vs, outs = [], []
        for f in range(F):
            v, out = chunk_apply(coeffs, y, f, x + 1, r)
            for q in range(Q):
                z[f, x, q, pl.ds(r, 8), :] = out[q] - v[q]
            vs.append(v)
            outs.append(out)
        add_gram(acc, 20, vs, outs)

    chunk_loop(chunk)


def edge_grams(b, y, acc, x):
    def chunk(r):
        vs = [tiles_of(b, (f, x), r + TOP) for f in range(F)]
        outs = [tiles_of(y, (f, x + 1), r + TOP) for f in range(F)]
        add_gram(acc, 0, vs, outs)
        add_gram(acc, 10, outs, outs)

    chunk_loop(chunk)


def inner_kernel(b, h, own, r0, r1, y_in, y, z, acc, tmp):
    del y_in
    par = lax.axis_index("gx") % 2
    ypar = lax.axis_index("gy") % 2
    far = side_planes(par)[0]
    acc[...] = jnp.zeros(acc.shape, jnp.float32)
    for side in range(2):
        row_halo(own, lambda item: halo_select(ypar, r0, r1, item)[side], side, y, tmp)

    def y_plane(x, carry):
        def chunk(r):
            coeffs = chunk_coeffs(h, x + 1, r)
            vs, outs = [], []
            for f in range(F):
                v, out = chunk_apply(coeffs, b, f, x, r)
                for q in range(Q):
                    y[f, x + 1, q, pl.ds(r + TOP, 8), :] = out[q]
                vs.append(v)
                outs.append(out)
            add_gram(acc, 0, vs, outs)
            add_gram(acc, 10, outs, outs)

        chunk_loop(chunk)
        return carry

    lax.fori_loop(1, NX - 1, y_plane, 0)
    edge_grams(b, y, acc, far)

    def z_loop(n, carry):
        z_plane(h, y, z, acc, jnp.where(par == 0, n, NX - 1 - n))
        return carry

    lax.fori_loop(1, NX - 2, z_loop, 0)


def inner(b, h, own, r0, r1, y):
    return pl.pallas_call(
        inner_kernel,
        out_shape=(
            f32(F, NX + 2, Q, ROWS, 128),
            f32(F, NX, Q, NY, 128),
            f32(30, 8, 128),
        ),
        in_specs=[VM] * 6,
        out_specs=(VM,) * 3,
        input_output_aliases={5: 0},
        scratch_shapes=[pltpu.VMEM((2, F, Q, 8, 128), jnp.float32)],
        compiler_params=params(),
        cost_estimate=cost(6),
        name="inner",
    )(b, h, own, r0, r1, y)


def halo_image(b, h, y, first, second, s0, x, halo):
    count_x, count_y = lax.axis_size("gx"), lax.axis_size("gy")
    ax, ay = lax.axis_index("gx"), lax.axis_index("gy")
    valid = jnp.where(x == 0, ax > 0, ax < count_x - 1)

    def chunk(r):
        for q in range(Q):
            c = h[x + 1, q, pl.ds(r + TOP, 8), :] + h[halo, q, pl.ds(r + TOP, 8), :]
            for f in range(F):
                a = (f * Q + q) * NY + r
                flux = c * (b[f, x, q, pl.ds(r + TOP, 8), :] - first[pl.ds(a, 8), :])
                other = second[pl.ds(s0 + a, 8), :] - flux
                y[f, halo, q, pl.ds(r + TOP, 8), :] = jnp.where(valid, other, 0.0)

    chunk_loop(chunk)
    for side in range(2):
        row = TOP - 1 if side == 0 else TOP + NY
        valid_row = ay > 0 if side == 0 else ay < count_y - 1
        base = s0 + F * PLANE + side * CORNER
        for q in range(Q):
            h_r = h[x + 1, q, row : row + 1, :]
            a = base + F * Q + q
            c = h_r + inside(second[a : a + 1, :], h_r)
            for f in range(F):
                v = b[f, x, q, row : row + 1, :]
                a = base + f * Q + q
                flux = jnp.where(valid_row, c * (v - second[a : a + 1, :]), 0.0)
                y[f, x + 1, q, row : row + 1, :] = y[f, x + 1, q, row : row + 1, :] + flux


def near_kernel(b, h_in, rin, y_in, z_in, acc_in, h, y, z, acc):
    del h_in, y_in, z_in
    par = lax.axis_index("gx") % 2
    _, near, _, halo = side_planes(par)
    acc[...] = acc_in[...]
    border(b, h, y, rin, near, halo)
    halo_image(b, h, y, rin, rin, L1_ROWS, near, halo)
    edge_grams(b, y, acc, near)

    def z_loop(n, carry):
        z_plane(h, y, z, acc, jnp.where(par == 0, n, NX - 1 - n))
        return carry

    lax.fori_loop(NX - 2, NX, z_loop, 0)


def near_side(b, h, rin, y, z, acc):
    return pl.pallas_call(
        near_kernel,
        out_shape=(
            f32(NX + 2, Q, ROWS, 128),
            f32(F, NX + 2, Q, ROWS, 128),
            f32(F, NX, Q, NY, 128),
            f32(30, 8, 128),
        ),
        in_specs=[VM] * 6,
        out_specs=(VM,) * 4,
        input_output_aliases={1: 0, 3: 1, 4: 2},
        compiler_params=params(),
        cost_estimate=cost(3),
        name="near",
    )(b, h, rin, y, z, acc)


def far_kernel(b, h, rl1, rl2, y_in, z_in, accb, acc_in, y, z, msg, acc):
    del y_in, z_in
    par = lax.axis_index("gx") % 2
    far, _, halo, _ = side_planes(par)
    acc[...] = acc_in[...]
    halo_image(b, h, y, rl1, rl2, 0, far, halo)
    z_plane(h, y, z, acc, far)
    sums = jnp.concatenate(
        [jnp.sum(accb[k], axis=0, keepdims=True) for k in range(10)]
        + [jnp.sum(acc[k], axis=0, keepdims=True) for k in range(30)]
        + [jnp.zeros((88, 128), jnp.float32)],
        axis=0,
    )
    msg[...] = lax.dot_general(
        jnp.ones((8, 128), jnp.float32),
        sums,
        (((1,), (1,)), ((), ())),
        precision=lax.Precision.HIGHEST,
        preferred_element_type=jnp.float32,
    )


def far_side(b, h, rl1, rl2, y, z, accb, acc):
    return pl.pallas_call(
        far_kernel,
        out_shape=(f32(F, NX + 2, Q, ROWS, 128), f32(F, NX, Q, NY, 128), f32(8, 128)),
        in_specs=[VM] * 8,
        out_specs=(VM,) * 3,
        input_output_aliases={4: 0, 5: 1},
        scratch_shapes=[pltpu.VMEM((30, 8, 128), jnp.float32)],
        compiler_params=params(),
        cost_estimate=cost(3),
        name="far",
    )(b, h, rl1, rl2, y, z, accb, acc)


def mm(a, b, ta=False):
    at = (lambda i, k: a[k][i]) if ta else (lambda i, k: a[i][k])
    return [
        [sum((at(i, k) * b[k][j] for k in range(1, F)), at(i, 0) * b[0][j]) for j in range(F)]
        for i in range(F)
    ]


def add(a, b, s=1.0):
    return [[a[i][j] + s * b[i][j] for j in range(F)] for i in range(F)]


def symmetric(a):
    return [[a[i][j] if i == j else 0.5 * (a[i][j] + a[j][i]) for j in range(F)] for i in range(F)]


def spd_solve(a, b):
    low = [[None] * F for _ in range(F)]
    d, inv = [None] * F, [None] * F
    for j in range(F):
        t = a[j][j]
        for k in range(j):
            t = t - low[j][k] * low[j][k] * d[k]
        d[j] = t
        inv[j] = 1.0 / t
        for i in range(j + 1, F):
            t = a[i][j]
            for k in range(j):
                t = t - low[i][k] * low[j][k] * d[k]
            low[i][j] = t * inv[j]
    x = [list(row) for row in b]
    for i in range(F):
        for k in range(i):
            for j in range(F):
                x[i][j] = x[i][j] - low[i][k] * x[k][j]
    for i in range(F):
        x[i] = [e * inv[i] for e in x[i]]
    for i in reversed(range(F)):
        for k in range(i + 1, F):
            for j in range(F):
                x[i][j] = x[i][j] - low[k][i] * x[k][j]
    return x


def step_matrices(entry):
    grams = []
    for g in range(4):
        m = [[None] * F for _ in range(F)]
        for n, (i, j) in enumerate(PAIRS):
            m[i][j] = m[j][i] = entry(10 * g + n)
        grams.append(m)
    bb, by, yy, yz = grams
    alpha = spd_solve(by, bb)
    new = symmetric(add(mm(alpha, mm(yy, alpha), ta=True), bb, -1.0))
    beta = spd_solve(bb, new)
    e = [[beta[i][j] + 1.0 if i == j else beta[i][j] for j in range(F)] for i in range(F)]
    cross = mm(e, mm(yy, alpha), ta=True)
    curv = add(mm(e, mm(by, e), ta=True), mm(alpha, mm(yz, alpha), ta=True))
    curv = [[curv[i][j] - cross[i][j] - cross[j][i] for j in range(F)] for i in range(F)]
    alpha2 = spd_solve(symmetric(curv), new)
    m1 = add(alpha, mm(e, alpha2))
    m2 = mm(alpha, alpha2)
    return m1, m2


def final_kernel(w, b, y, d, xs_out, res_out, coef):
    x = pl.program_id(0)

    @pl.when(x == 0)
    def _():
        total = jnp.sum(w[...], axis=0, keepdims=True)
        sub = lax.broadcasted_iota(jnp.int32, (128, 128), 0)
        lane = lax.broadcasted_iota(jnp.int32, (128, 128), 1)
        spread = lax.dot_general(
            jnp.where(sub == lane, total, 0.0),
            jnp.ones((128, 128), jnp.float32),
            (((1,), (0,)), ((), ())),
            precision=lax.Precision.HIGHEST,
            preferred_element_type=jnp.float32,
        )
        m1, m2 = step_matrices(lambda k: spread[k : k + 1, :])
        for i in range(F):
            for j in range(F):
                n = i * F + j
                coef[n] = jnp.broadcast_to(m1[i][j], (8, 128))
                coef[16 + n] = jnp.broadcast_to(m2[i][j], (8, 128))
                coef[32 + n] = jnp.broadcast_to(m1[i][j] - m2[i][j], (8, 128))

    def body(i, carry):
        r = pl.multiple_of(i * 8, 8)
        for q in range(Q):
            bs = [b[f, x, q, pl.ds(r + TOP, 8), :] for f in range(F)]
            ys = [y[f, x + 1, q, pl.ds(r + TOP, 8), :] for f in range(F)]
            ds = [d[f, x, q, pl.ds(r, 8), :] for f in range(F)]
            es = [bs[f] - ys[f] for f in range(F)]
            for j in range(F):
                p = ys[0] * coef[32 + j]
                for k in range(1, F):
                    p = p + ys[k] * coef[32 + k * F + j]
                ro = bs[j] - p
                for k in range(F):
                    p = p + es[k] * coef[k * F + j]
                    ro = ro + ds[k] * coef[16 + k * F + j]
                s = slice(q * 128, q * 128 + 128)
                xs_out[j, 0, pl.ds(r, 8), s] = p
                res_out[j, 0, pl.ds(r, 8), s] = ro
        return carry

    lax.fori_loop(0, CHUNKS, body, 0)


def final(w, b, y, d):
    block = pl.BlockSpec((F, 1, NY, NZ), lambda x: (0, x, 0, 0))
    out = jax.ShapeDtypeStruct((F, NX, NY, NZ), jnp.float32)
    return pl.pallas_call(
        final_kernel,
        grid=(NX,),
        out_shape=(out, out),
        in_specs=[VM] * 4,
        out_specs=(block, block),
        scratch_shapes=[pltpu.VMEM((48, 8, 128), jnp.float32)],
        compiler_params=params(),
        cost_estimate=cost(5),
        name="final",
    )(w, b, y, d)


def exchange(x, sizes, partner):
    nx, ny = sizes
    pairs = []
    for a in range(nx):
        for c in range(ny):
            ta, tc = partner(a, c)
            if 0 <= ta < nx and 0 <= tc < ny:
                pairs.append((a * ny + c, ta * ny + tc))
    return lax.ppermute(x, AXES, pairs)


def shards(sizes, adjoint_source, conductivity, electrodes):
    nx, ny = sizes
    current = math.sqrt(nx * NX * ny * NY * NZ)
    border_pair = lambda a, c: (a + 1 if a % 2 else a - 1, c)
    inputs = (current, adjoint_source, conductivity, electrodes)
    l1, g0, g1, own = pack(*inputs)
    rl1 = exchange(l1, sizes, border_pair)
    r0 = exchange(g0, sizes, lambda a, c: (a, c ^ 1))
    r1 = exchange(g1, sizes, lambda a, c: (a, c + 1 if c % 2 else c - 1))
    b, h, accb = load_fields(*inputs)
    b, h, y, l2, intra = edge(b, h, own, r0, r1, rl1)
    rl2 = exchange(l2, sizes, border_pair)
    rin = exchange(intra, sizes, lambda a, c: (a ^ 1, c))
    y, z, acc = inner(b, h, own, r0, r1, y)
    h, y, z, acc = near_side(b, h, rin, y, z, acc)
    y, z, msg = far_side(b, h, rl1, rl2, y, z, accb, acc)
    sent = jnp.broadcast_to(msg[0:1][None], (nx * ny, 1, 128))
    w = lax.all_to_all(sent, AXES, 0, 0).reshape(nx * ny, 128)
    return final(w, b, y, z)


def solution(mesh):
    sizes = (mesh.shape["gx"], mesh.shape["gy"])
    placed = (P(None, "gx", "gy", None), P("gx", "gy", None), P())
    return jax.shard_map(
        functools.partial(shards, sizes),
        mesh=mesh,
        in_specs=placed,
        out_specs=(P(None, "gx", "gy", None), P(None, "gx", "gy", None)),
        check_vma=False,
    )
```

```python
import functools
import math

import jax
import jax.numpy as jnp
from jax import lax
from jax.experimental import pallas as pl
from jax.experimental.pallas import tpu as pltpu
from jax.sharding import PartitionSpec as P

AXES = ("gx", "gy")
F = 4
NX = 8
NY = 64
NZ = 512
Q = NZ // 128
CHUNKS = NY // 8
UNROLL = 4
PAIRS = [(i, j) for i in range(F) for j in range(i, F)]
TOP = 8
ROWS = NY + 2 * TOP
PLANE = Q * NY
L1_ROWS = (F + 1) * PLANE
CORNER = 24
L2_ROWS = F * PLANE + 2 * CORNER
IN_ROWS = L1_ROWS + L2_ROWS
TILE_ROWS = (F + 1) * Q * 8
G_ROWS = TILE_ROWS + F * Q * 8
VMEM_LIMIT = 16 * 1024 * 1024

VM = pl.BlockSpec(memory_space=pltpu.VMEM)
HBM = pl.BlockSpec(memory_space=pltpu.HBM)


def f32(*shape):
    return pltpu.VMEM(shape, jnp.float32)


def params():
    return pltpu.CompilerParams(vmem_limit_bytes=VMEM_LIMIT)


def cost(us):
    return pl.CostEstimate(flops=int(us * 4e6), bytes_accessed=int(us * 3.0e6), transcendentals=0)


def in_hbm(*arrays):
    return tuple(pltpu.with_memory_space_constraint(a, pltpu.HBM) for a in arrays)


def iota(dim):
    return lax.broadcasted_iota(jnp.int32, (8, 128), dim)


def inside(h_other, h):
    return jnp.where(h_other > 0.0, h_other, h)


def above_z(v):
    t = [pltpu.roll(a, 127, 1) for a in v]
    last = iota(1) == 127
    return [jnp.where(last, t[q + 1], t[q]) if q < Q - 1 else t[q] for q in range(Q)]


def below_z(v):
    t = [pltpu.roll(a, 1, 1) for a in v]
    first = iota(1) == 0
    return [jnp.where(first, t[q - 1], t[q]) if q > 0 else t[q] for q in range(Q)]


def z_coeffs(h):
    up = [a + b for a, b in zip(h, above_z(h))]
    down = [a + b for a, b in zip(h, below_z(h))]
    first, last = iota(1) == 0, iota(1) == 127
    total = [a + b for a, b in zip(up, down)]
    total[0] = up[0] + jnp.where(first, 2.0 * h[0], down[0])
    total[-1] = jnp.where(last, 2.0 * h[-1], up[-1]) + down[-1]
    down[0] = jnp.where(first, 0.0, down[0])
    up[-1] = jnp.where(last, 0.0, up[-1])
    return up, down, total


def add_gram(acc, base, left, right):
    for n, (i, j) in enumerate(PAIRS):
        t = left[i][0] * right[j][0]
        for q in range(1, Q):
            t = t + left[i][q] * right[j][q]
        acc[base + n] += t


def chunk_loop(body):
    def step(i, carry):
        for u in range(UNROLL):
            body(pl.multiple_of(i * (8 * UNROLL), 8) + 8 * u)
        return carry

    lax.fori_loop(0, CHUNKS // UNROLL, step, 0)


def tiles_of(ref, index, row):
    return [ref[(*index, q, pl.ds(row, 8), slice(None))] for q in range(Q)]


def add_spike(ref, index, row, current):
    tile = ref[(*index, slice(0, 128))]
    ref[(*index, slice(0, 128))] = tile + jnp.where(
        (iota(0) == row) & (iota(1) == 0), current, 0.0
    )


def local_cell(elec, f):
    total_y = NY * lax.axis_size("gy")
    cell = elec[f]
    lx = cell // total_y - lax.axis_index("gx") * NX
    ly = cell % total_y - lax.axis_index("gy") * NY
    return lx, ly, (lx >= 0) & (lx < NX) & (ly >= 0) & (ly < NY)


def pack_kernel(
    current, adj, sigma, elec_in, l1_out, g0_out, g1_out, own_out, plane, tiles, far_rows, elec, sems, esem
):
    par = lax.axis_index("gx") % 2
    ypar = lax.axis_index("gy") % 2
    edge = par * (NX - 1)
    ecopy = pltpu.make_async_copy(elec_in, elec, esem)
    ecopy.start()
    copies = []
    for f in range(F + 1):
        src = adj.at[f] if f < F else sigma
        copies.append(pltpu.make_async_copy(src.at[edge], plane.at[f], sems.at[0, f]))
        for side, y in ((0, 0), (1, NY - 8)):
            copies.append(
                pltpu.make_async_copy(
                    src.at[:, pl.ds(y, 8), :], tiles.at[f, side], sems.at[1 + side, f]
                )
            )
    for c in copies:
        c.start()
    ecopy.wait()
    for c in copies:
        c.wait()
    for f in range(F):
        lx, ly, here = local_cell(elec, f)

        @pl.when(here & (lx == edge))
        def _(f=f, ly=ly):
            r8 = pl.multiple_of((ly // 8) * 8, 8)
            add_spike(plane, (f, pl.ds(r8, 8)), ly - r8, current)

        @pl.when(here & (ly < 8))
        def _(f=f, lx=lx, ly=ly):
            add_spike(tiles, (f, 0, lx, slice(0, 8)), ly, current)

        @pl.when(here & (ly >= NY - 8))
        def _(f=f, lx=lx, ly=ly):
            add_spike(tiles, (f, 1, lx, slice(0, 8)), ly - (NY - 8), current)

    for f in range(F + 1):
        k = 1.0 if f < F else 0.5
        for q in range(Q):
            s = slice(q * 128, q * 128 + 128)
            a = (f * Q + q) * NY
            l1_out[a : a + NY, :] = k * plane[f, :, s]
            for x in range(NX):
                a = (f * Q + q) * 8 + x
                for side, (near, far) in enumerate(((0, 1), (7, 6))):
                    own_out[side, a : a + 1, :] = k * tiles[f, side, x, near : near + 1, s]
                    far_rows[side, a : a + 1, :] = k * tiles[f, side, x, far : far + 1, s]
    for f in range(F + 1):
        for q in range(Q):
            t = slice((f * Q + q) * 8, (f * Q + q) * 8 + 8)
            lo, hi = own_out[0, t, :], own_out[1, t, :]
            g0_out[t, :] = jnp.where(ypar == 0, hi, lo)
            g1_out[t, :] = jnp.where(ypar == 0, lo, hi)
            if f < F:
                ht = slice((F * Q + q) * 8, (F * Q + q) * 8 + 8)
                lo = (own_out[0, ht, :] + far_rows[0, ht, :]) * (lo - far_rows[0, t, :])
                hi = (own_out[1, ht, :] + far_rows[1, ht, :]) * (hi - far_rows[1, t, :])
                d = slice(TILE_ROWS + (f * Q + q) * 8, TILE_ROWS + (f * Q + q) * 8 + 8)
                g0_out[d, :] = jnp.where(ypar == 0, hi, lo)
                g1_out[d, :] = jnp.where(ypar == 0, lo, hi)


def pack(current, adj, sigma, electrodes):
    return pl.pallas_call(
        functools.partial(pack_kernel, current),
        out_shape=(
            f32(L1_ROWS, 128),
            f32(G_ROWS, 128),
            f32(G_ROWS, 128),
            f32(2, TILE_ROWS, 128),
        ),
        in_specs=[HBM] * 3,
        out_specs=(VM,) * 4,
        scratch_shapes=[
            pltpu.VMEM((F + 1, NY, NZ), jnp.float32),
            pltpu.VMEM((F + 1, 2, NX, 8, NZ), jnp.float32),
            pltpu.VMEM((2, TILE_ROWS, 128), jnp.float32),
            pltpu.SMEM((F,), jnp.int32),
            pltpu.SemaphoreType.DMA((3, F + 1)),
            pltpu.SemaphoreType.DMA,
        ],
        compiler_params=params(),
        cost_estimate=cost(2),
        name="pack",
    )(*in_hbm(adj, sigma, electrodes))


def load_kernel(current, adj, sigma, elec_in, b_out, h_out, acc, fields, cond, elec, sems, esem):
    ecopy = pltpu.make_async_copy(elec_in, elec, esem)
    ecopy.start()
    copies = [pltpu.make_async_copy(adj.at[f], fields.at[f], sems.at[f]) for f in range(F)]
    copies.append(pltpu.make_async_copy(sigma, cond, sems.at[F]))
    for c in copies:
        c.start()
    ecopy.wait()
    acc[...] = jnp.zeros(acc.shape, jnp.float32)
    for c in copies:
        c.wait()
    for f in range(F):
        lx, ly, here = local_cell(elec, f)

        @pl.when(here)
        def _(f=f, lx=lx, ly=ly):
            r8 = pl.multiple_of((ly // 8) * 8, 8)
            add_spike(fields, (f, lx, pl.ds(r8, 8)), ly - r8, current)

    def plane(x, carry):
        def chunk(r):
            vs = []
            for f in range(F):
                v = [fields[f, x, pl.ds(r, 8), q * 128 : q * 128 + 128] for q in range(Q)]
                for q in range(Q):
                    b_out[f, x, q, pl.ds(r + TOP, 8), :] = v[q]
                vs.append(v)
            for q in range(Q):
                h_out[x + 1, q, pl.ds(r + TOP, 8), :] = (
                    0.5 * cond[x, pl.ds(r, 8), q * 128 : q * 128 + 128]
                )
            add_gram(acc, 0, vs, vs)

        chunk_loop(chunk)
        return carry

    lax.fori_loop(0, NX, plane, 0)


def load_fields(current, adj, sigma, electrodes):
    return pl.pallas_call(
        functools.partial(load_kernel, current),
        out_shape=(f32(F, NX, Q, ROWS, 128), f32(NX + 2, Q, ROWS, 128), f32(10, 8, 128)),
        in_specs=[HBM] * 3,
        out_specs=(VM,) * 3,
        scratch_shapes=[
            pltpu.VMEM((F, NX, NY, NZ), jnp.float32),
            pltpu.VMEM((NX, NY, NZ), jnp.float32),
            pltpu.SMEM((F,), jnp.int32),
            pltpu.SemaphoreType.DMA((F + 1,)),
            pltpu.SemaphoreType.DMA,
        ],
        compiler_params=params(),
        cost_estimate=cost(3),
        name="load",
    )(*in_hbm(adj, sigma, electrodes))


def chunk_coeffs(h, k, r, low=True, high=True):
    at = r + TOP
    own = tiles_of(h, (k,), at)
    up, down, total = z_coeffs(own)
    faces = [(None, up), (None, down)]
    others = [((0, 1), tiles_of(h, (k,), at + 1)), ((0, -1), tiles_of(h, (k,), at - 1))]
    if low:
        others.append(((-1, 0), tiles_of(h, (k - 1,), at)))
    if high:
        others.append(((1, 0), tiles_of(h, (k + 1,), at)))
    for step, other in others:
        c = [a + b for a, b in zip(own, other)]
        total = [a + b for a, b in zip(total, c)]
        faces.append((step, c))
    return total, faces


def chunk_apply(coeffs, v, f, k, r):
    total, faces = coeffs
    at = r + TOP
    own = tiles_of(v, (f, k), at)
    out = []
    up, down = above_z(own), below_z(own)
    for q in range(Q):
        t = total[q] * own[q] - faces[0][1][q] * up[q] - faces[1][1][q] * down[q]
        u = None
        for s, c in faces[2:]:
            n = c[q] * v[f, k + s[0], q, pl.ds(at + s[1], 8), :]
            u = n if u is None else u + n
        out.append(t - u)
    return own, out


def side_planes(par):
    far = par * (NX - 1)
    near = (NX - 1) - far
    return far, near, par * (NX + 1), (1 - par) * (NX + 1)


def halo_select(ypar, r0, r1, item):
    a = r0[item * 8 : item * 8 + 8, :]
    b = r1[item * 8 : item * 8 + 8, :]
    return jnp.where(ypar == 0, b, a), jnp.where(ypar == 0, a, b)


def edge_kernel(b_in, h_in, own, r0, r1, rl1, b, h, y, l2_out, in_out, g):
    del b_in, h_in
    par = lax.axis_index("gx") % 2
    ypar = lax.axis_index("gy") % 2
    far, near, far_halo, _ = side_planes(par)
    for item in range((F + 1) * Q):
        f, q = divmod(item, Q)
        for side, t in enumerate(halo_select(ypar, r0, r1, item)):
            row = TOP - 1 if side == 0 else TOP + NY
            g[side, item * 8 : item * 8 + 8, :] = t
            if f < F:
                for x in range(NX):
                    b[f, x, q, row : row + 1, :] = g[side, item * 8 + x : item * 8 + x + 1, :]
            else:
                t = inside(t, own[side, item * 8 : item * 8 + 8, :])
                g[2 + side, q * 8 : q * 8 + 8, :] = t
                for x in range(NX):
                    h[x + 1, q, row : row + 1, :] = g[2 + side, q * 8 + x : q * 8 + x + 1, :]
    for x in (0, NX - 1):

        def chunk(r, x=x):
            coeffs = chunk_coeffs(h, x + 1, r, low=x > 0, high=x == 0)
            for f in range(F):
                _, out = chunk_apply(coeffs, b, f, x, r)
                for q in range(Q):
                    y[f, x + 1, q, pl.ds(r + TOP, 8), :] = out[q]

        chunk_loop(chunk)
    data = slice(TOP, TOP + NY)
    for q in range(Q):
        for f in range(F):
            a = (f * Q + q) * NY
            l2_out[a : a + NY, :] = y[f, far + 1, q, data, :]
            in_out[a : a + NY, :] = b[f, near, q, data, :]
            in_out[L1_ROWS + a : L1_ROWS + a + NY, :] = y[f, near + 1, q, data, :]
        a = (F * Q + q) * NY
        in_out[a : a + NY, :] = h[near + 1, q, data, :]
    base = F * PLANE
    l2_out[base:L2_ROWS, :] = jnp.zeros((2 * CORNER, 128), jnp.float32)
    in_out[L1_ROWS + base : IN_ROWS, :] = jnp.zeros((2 * CORNER, 128), jnp.float32)
    for side in range(2):
        for item in range((F + 1) * Q):
            a = base + side * CORNER + item
            l2_out[a : a + 1, :] = g[side, pl.ds(item * 8 + far, 1), :]
            in_out[L1_ROWS + a : L1_ROWS + a + 1, :] = g[side, pl.ds(item * 8 + near, 1), :]
    border(b, h, y, rl1, far, far_halo)


def border(b, h, y, first, x, halo):
    def chunk(r):
        for q in range(Q):
            own = h[x + 1, q, pl.ds(r + TOP, 8), :]
            beyond = inside(first[pl.ds((F * Q + q) * NY + r, 8), :], own)
            h[halo, q, pl.ds(r + TOP, 8), :] = beyond
            c = own + beyond
            for f in range(F):
                v = b[f, x, q, pl.ds(r + TOP, 8), :]
                flux = c * (v - first[pl.ds((f * Q + q) * NY + r, 8), :])
                at = (f, x + 1, q, pl.ds(r + TOP, 8), slice(None))
                y[at] = y[at] + flux

    chunk_loop(chunk)


def edge(b, h, own, r0, r1, rl1):
    return pl.pallas_call(
        edge_kernel,
        out_shape=(
            f32(F, NX, Q, ROWS, 128),
            f32(NX + 2, Q, ROWS, 128),
            f32(F, NX + 2, Q, ROWS, 128),
            f32(L2_ROWS, 128),
            f32(IN_ROWS, 128),
        ),
        in_specs=[VM] * 6,
        out_specs=(VM,) * 5,
        input_output_aliases={0: 0, 1: 1},
        scratch_shapes=[pltpu.VMEM((4, TILE_ROWS, 128), jnp.float32)],
        compiler_params=params(),
        cost_estimate=cost(10),
        name="edge",
    )(b, h, own, r0, r1, rl1)


def row_halo(own, rh, side, y, tmp):
    count = lax.axis_size("gy")
    ay = lax.axis_index("gy")
    valid = ay > 0 if side == 0 else ay < count - 1
    row = TOP - 1 if side == 0 else TOP + NY
    sub = iota(0)
    own_at = lambda f, q: own[side, (f * Q + q) * 8 : (f * Q + q) * 8 + 8, :]
    h_r = [rh(F * Q + q) for q in range(Q)]
    zu, zd, total = z_coeffs(h_r)
    across = [h_r[q] + own_at(F, q) for q in range(Q)]
    up = [jnp.where(sub == NX - 1, 0.0, a + pltpu.roll(a, 7, 0)) for a in h_r]
    down = [jnp.where(sub == 0, 0.0, a + pltpu.roll(a, 1, 0)) for a in h_r]
    total = [sum(t) for t in zip(total, across, up, down)]
    for f in range(F):
        v = [rh(f * Q + q) for q in range(Q)]
        zp, zm = above_z(v), below_z(v)
        for q in range(Q):
            out = total[q] * v[q] + rh((F + 1 + f) * Q + q) - across[q] * own_at(f, q)
            out = out - up[q] * pltpu.roll(v[q], 7, 0) - down[q] * pltpu.roll(v[q], 1, 0)
            out = out - zu[q] * zp[q] - zd[q] * zm[q]
            tmp[side, f, q] = jnp.where(valid, out, 0.0)
            for x in range(NX):
                y[f, x + 1, q, row : row + 1, :] = tmp[side, f, q, x : x + 1, :]


def z_plane(h, y, d, acc, x):
    def chunk(r):
        coeffs = chunk_coeffs(h, x + 1, r)
        for f in range(F):
            v, out = chunk_apply(coeffs, y, f, x + 1, r)
            for q in range(Q):
                d[f, x, q, pl.ds(r, 8), :] = out[q] - v[q]

    def grams(r):
        ys = [tiles_of(y, (f, x + 1), r + TOP) for f in range(F)]
        add_gram(acc, 20, ys, [tiles_of(d, (f, x), r) for f in range(F)])

    chunk_loop(chunk)
    chunk_loop(grams)


def plane_grams(b, y, acc, x):
    def chunk(r):
        vs = [tiles_of(b, (f, x), r + TOP) for f in range(F)]
        outs = [tiles_of(y, (f, x + 1), r + TOP) for f in range(F)]
        add_gram(acc, 0, vs, outs)
        add_gram(acc, 10, outs, outs)

    chunk_loop(chunk)


def inner_kernel(b, h, own, r0, r1, y_in, y, z, acc, tmp):
    del y_in
    par = lax.axis_index("gx") % 2
    ypar = lax.axis_index("gy") % 2
    far = side_planes(par)[0]
    acc[...] = jnp.zeros(acc.shape, jnp.float32)
    for side in range(2):
        row_halo(own, lambda item: halo_select(ypar, r0, r1, item)[side], side, y, tmp)

    def y_plane(x, carry):
        def chunk(r):
            coeffs = chunk_coeffs(h, x + 1, r)
            for f in range(F):
                _, out = chunk_apply(coeffs, b, f, x, r)
                for q in range(Q):
                    y[f, x + 1, q, pl.ds(r + TOP, 8), :] = out[q]

        chunk_loop(chunk)
        plane_grams(b, y, acc, x)
        return carry

    lax.fori_loop(1, NX - 1, y_plane, 0)
    plane_grams(b, y, acc, far)

    def z_loop(n, carry):
        z_plane(h, y, z, acc, jnp.where(par == 0, n, NX - 1 - n))
        return carry

    lax.fori_loop(1, NX - 2, z_loop, 0)


def inner(b, h, own, r0, r1, y):
    return pl.pallas_call(
        inner_kernel,
        out_shape=(
            f32(F, NX + 2, Q, ROWS, 128),
            f32(F, NX, Q, NY, 128),
            f32(30, 8, 128),
        ),
        in_specs=[VM] * 6,
        out_specs=(VM,) * 3,
        input_output_aliases={5: 0},
        scratch_shapes=[pltpu.VMEM((2, F, Q, 8, 128), jnp.float32)],
        compiler_params=params(),
        cost_estimate=cost(6),
        name="inner",
    )(b, h, own, r0, r1, y)


def halo_image(b, h, y, first, second, s0, x, halo):
    count_x, count_y = lax.axis_size("gx"), lax.axis_size("gy")
    ax, ay = lax.axis_index("gx"), lax.axis_index("gy")
    valid = jnp.where(x == 0, ax > 0, ax < count_x - 1)

    def chunk(r):
        for q in range(Q):
            c = h[x + 1, q, pl.ds(r + TOP, 8), :] + h[halo, q, pl.ds(r + TOP, 8), :]
            for f in range(F):
                a = (f * Q + q) * NY + r
                flux = c * (b[f, x, q, pl.ds(r + TOP, 8), :] - first[pl.ds(a, 8), :])
                other = second[pl.ds(s0 + a, 8), :] - flux
                y[f, halo, q, pl.ds(r + TOP, 8), :] = jnp.where(valid, other, 0.0)

    chunk_loop(chunk)
    for side in range(2):
        row = TOP - 1 if side == 0 else TOP + NY
        valid_row = ay > 0 if side == 0 else ay < count_y - 1
        base = s0 + F * PLANE + side * CORNER
        for q in range(Q):
            h_r = h[x + 1, q, row : row + 1, :]
            a = base + F * Q + q
            c = h_r + inside(second[a : a + 1, :], h_r)
            for f in range(F):
                v = b[f, x, q, row : row + 1, :]
                a = base + f * Q + q
                flux = jnp.where(valid_row, c * (v - second[a : a + 1, :]), 0.0)
                y[f, x + 1, q, row : row + 1, :] = y[f, x + 1, q, row : row + 1, :] + flux


def near_kernel(b, h_in, rin, y_in, z_in, acc_in, h, y, z, acc):
    del h_in, y_in, z_in
    par = lax.axis_index("gx") % 2
    _, near, _, halo = side_planes(par)
    acc[...] = acc_in[...]
    border(b, h, y, rin, near, halo)
    halo_image(b, h, y, rin, rin, L1_ROWS, near, halo)
    plane_grams(b, y, acc, near)

    def z_loop(n, carry):
        z_plane(h, y, z, acc, jnp.where(par == 0, n, NX - 1 - n))
        return carry

    lax.fori_loop(NX - 2, NX, z_loop, 0)


def near_side(b, h, rin, y, z, acc):
    return pl.pallas_call(
        near_kernel,
        out_shape=(
            f32(NX + 2, Q, ROWS, 128),
            f32(F, NX + 2, Q, ROWS, 128),
            f32(F, NX, Q, NY, 128),
            f32(30, 8, 128),
        ),
        in_specs=[VM] * 6,
        out_specs=(VM,) * 4,
        input_output_aliases={1: 0, 3: 1, 4: 2},
        compiler_params=params(),
        cost_estimate=cost(3),
        name="near",
    )(b, h, rin, y, z, acc)


def far_kernel(b, h, rl1, rl2, y_in, z_in, accb, acc_in, y, z, msg, acc):
    del y_in, z_in
    par = lax.axis_index("gx") % 2
    far, _, halo, _ = side_planes(par)
    acc[...] = acc_in[...]
    halo_image(b, h, y, rl1, rl2, 0, far, halo)
    z_plane(h, y, z, acc, far)
    sums = jnp.concatenate(
        [jnp.sum(accb[k], axis=0, keepdims=True) for k in range(10)]
        + [jnp.sum(acc[k], axis=0, keepdims=True) for k in range(30)]
        + [jnp.zeros((88, 128), jnp.float32)],
        axis=0,
    )
    msg[...] = lax.dot_general(
        jnp.ones((8, 128), jnp.float32),
        sums,
        (((1,), (1,)), ((), ())),
        precision=lax.Precision.HIGHEST,
        preferred_element_type=jnp.float32,
    )


def far_side(b, h, rl1, rl2, y, z, accb, acc):
    return pl.pallas_call(
        far_kernel,
        out_shape=(f32(F, NX + 2, Q, ROWS, 128), f32(F, NX, Q, NY, 128), f32(8, 128)),
        in_specs=[VM] * 8,
        out_specs=(VM,) * 3,
        input_output_aliases={4: 0, 5: 1},
        scratch_shapes=[pltpu.VMEM((30, 8, 128), jnp.float32)],
        compiler_params=params(),
        cost_estimate=cost(3),
        name="far",
    )(b, h, rl1, rl2, y, z, accb, acc)


def mm(a, b, ta=False):
    at = (lambda i, k: a[k][i]) if ta else (lambda i, k: a[i][k])
    return [
        [sum((at(i, k) * b[k][j] for k in range(1, F)), at(i, 0) * b[0][j]) for j in range(F)]
        for i in range(F)
    ]


def add(a, b, s=1.0):
    return [[a[i][j] + s * b[i][j] for j in range(F)] for i in range(F)]


def symmetric(a):
    return [[a[i][j] if i == j else 0.5 * (a[i][j] + a[j][i]) for j in range(F)] for i in range(F)]


def spd_solve(a, b):
    low = [[None] * F for _ in range(F)]
    d, inv = [None] * F, [None] * F
    for j in range(F):
        t = a[j][j]
        for k in range(j):
            t = t - low[j][k] * low[j][k] * d[k]
        d[j] = t
        inv[j] = 1.0 / t
        for i in range(j + 1, F):
            t = a[i][j]
            for k in range(j):
                t = t - low[i][k] * low[j][k] * d[k]
            low[i][j] = t * inv[j]
    x = [list(row) for row in b]
    for i in range(F):
        for k in range(i):
            for j in range(F):
                x[i][j] = x[i][j] - low[i][k] * x[k][j]
    for i in range(F):
        x[i] = [e * inv[i] for e in x[i]]
    for i in reversed(range(F)):
        for k in range(i + 1, F):
            for j in range(F):
                x[i][j] = x[i][j] - low[k][i] * x[k][j]
    return x


def step_matrices(entry):
    grams = []
    for g in range(4):
        m = [[None] * F for _ in range(F)]
        for n, (i, j) in enumerate(PAIRS):
            m[i][j] = m[j][i] = entry(10 * g + n)
        grams.append(m)
    bb, by, yy, yd = grams
    yz = add(yd, yy)
    alpha = spd_solve(by, bb)
    new = symmetric(add(mm(alpha, mm(yy, alpha), ta=True), bb, -1.0))
    beta = spd_solve(bb, new)
    e = [[beta[i][j] + 1.0 if i == j else beta[i][j] for j in range(F)] for i in range(F)]
    cross = mm(e, mm(yy, alpha), ta=True)
    curv = add(mm(e, mm(by, e), ta=True), mm(alpha, mm(yz, alpha), ta=True))
    curv = [[curv[i][j] - cross[i][j] - cross[j][i] for j in range(F)] for i in range(F)]
    alpha2 = spd_solve(symmetric(curv), new)
    m1 = add(alpha, mm(e, alpha2))
    m2 = mm(alpha, alpha2)
    return m1, m2


def final_kernel(w, b, y, d, xs_out, res_out, coef):
    x = pl.program_id(0)

    @pl.when(x == 0)
    def _():
        total = jnp.sum(w[...], axis=0, keepdims=True)
        sub = lax.broadcasted_iota(jnp.int32, (128, 128), 0)
        lane = lax.broadcasted_iota(jnp.int32, (128, 128), 1)
        spread = lax.dot_general(
            jnp.where(sub == lane, total, 0.0),
            jnp.ones((128, 128), jnp.float32),
            (((1,), (0,)), ((), ())),
            precision=lax.Precision.HIGHEST,
            preferred_element_type=jnp.float32,
        )
        m1, m2 = step_matrices(lambda k: spread[k : k + 1, :])
        for i in range(F):
            for j in range(F):
                n = i * F + j
                coef[n] = jnp.broadcast_to(m1[i][j], (8, 128))
                coef[16 + n] = jnp.broadcast_to(m2[i][j], (8, 128))
                coef[32 + n] = jnp.broadcast_to(m1[i][j] - m2[i][j], (8, 128))

    def body(i, carry):
        r = pl.multiple_of(i * 8, 8)
        for q in range(Q):
            bs = [b[f, x, q, pl.ds(r + TOP, 8), :] for f in range(F)]
            ys = [y[f, x + 1, q, pl.ds(r + TOP, 8), :] for f in range(F)]
            ds = [d[f, x, q, pl.ds(r, 8), :] for f in range(F)]
            es = [bs[f] - ys[f] for f in range(F)]
            for j in range(F):
                p = ys[0] * coef[32 + j]
                for k in range(1, F):
                    p = p + ys[k] * coef[32 + k * F + j]
                ro = bs[j] - p
                for k in range(F):
                    p = p + es[k] * coef[k * F + j]
                    ro = ro + ds[k] * coef[16 + k * F + j]
                s = slice(q * 128, q * 128 + 128)
                xs_out[j, 0, pl.ds(r, 8), s] = p
                res_out[j, 0, pl.ds(r, 8), s] = ro
        return carry

    lax.fori_loop(0, CHUNKS, body, 0)


def final(w, b, y, d):
    block = pl.BlockSpec((F, 1, NY, NZ), lambda x: (0, x, 0, 0))
    out = jax.ShapeDtypeStruct((F, NX, NY, NZ), jnp.float32)
    return pl.pallas_call(
        final_kernel,
        grid=(NX,),
        out_shape=(out, out),
        in_specs=[VM] * 4,
        out_specs=(block, block),
        scratch_shapes=[pltpu.VMEM((48, 8, 128), jnp.float32)],
        compiler_params=params(),
        cost_estimate=cost(5),
        name="final",
    )(w, b, y, d)


def exchange(x, sizes, partner):
    nx, ny = sizes
    pairs = []
    for a in range(nx):
        for c in range(ny):
            ta, tc = partner(a, c)
            if 0 <= ta < nx and 0 <= tc < ny:
                pairs.append((a * ny + c, ta * ny + tc))
    return lax.ppermute(x, AXES, pairs)


def shards(sizes, adjoint_source, conductivity, electrodes):
    nx, ny = sizes
    current = math.sqrt(nx * NX * ny * NY * NZ)
    border_pair = lambda a, c: (a + 1 if a % 2 else a - 1, c)
    inputs = (current, adjoint_source, conductivity, electrodes)
    l1, g0, g1, own = pack(*inputs)
    rl1 = exchange(l1, sizes, border_pair)
    r0 = exchange(g0, sizes, lambda a, c: (a, c ^ 1))
    r1 = exchange(g1, sizes, lambda a, c: (a, c + 1 if c % 2 else c - 1))
    b, h, accb = load_fields(*inputs)
    b, h, y, l2, intra = edge(b, h, own, r0, r1, rl1)
    rl2 = exchange(l2, sizes, border_pair)
    rin = exchange(intra, sizes, lambda a, c: (a ^ 1, c))
    y, z, acc = inner(b, h, own, r0, r1, y)
    h, y, z, acc = near_side(b, h, rin, y, z, acc)
    y, z, msg = far_side(b, h, rl1, rl2, y, z, accb, acc)
    sent = jnp.broadcast_to(msg[0:1][None], (nx * ny, 1, 128))
    w = lax.all_to_all(sent, AXES, 0, 0).reshape(nx * ny, 128)
    return final(w, b, y, z)


def solution(mesh):
    sizes = (mesh.shape["gx"], mesh.shape["gy"])
    placed = (P(None, "gx", "gy", None), P("gx", "gy", None), P())
    return jax.shard_map(
        functools.partial(shards, sizes),
        mesh=mesh,
        in_specs=placed,
        out_specs=(P(None, "gx", "gy", None), P(None, "gx", "gy", None)),
        check_vma=False,
    )
```

```python
import functools
import math

import jax
import jax.numpy as jnp
from jax import lax
from jax.experimental import pallas as pl
from jax.experimental.pallas import tpu as pltpu
from jax.sharding import PartitionSpec as P

AXES = ("gx", "gy")
F = 4
NX = 8
NY = 64
NZ = 512
Q = NZ // 128
CHUNKS = NY // 8
UNROLL = 4
PAIRS = [(i, j) for i in range(F) for j in range(i, F)]
TOP = 8
ROWS = NY + 2 * TOP
PLANE = Q * NY
L1_ROWS = (F + 1) * PLANE
CORNER = 24
L2_ROWS = F * PLANE + 2 * CORNER
IN_ROWS = L1_ROWS + L2_ROWS
TILE_ROWS = (F + 1) * Q * 8
G_ROWS = TILE_ROWS + F * Q * 8
VMEM_LIMIT = 16 * 1024 * 1024

VM = pl.BlockSpec(memory_space=pltpu.VMEM)
HBM = pl.BlockSpec(memory_space=pltpu.HBM)


def f32(*shape):
    return pltpu.VMEM(shape, jnp.float32)


def params():
    return pltpu.CompilerParams(vmem_limit_bytes=VMEM_LIMIT)


def cost(us):
    return pl.CostEstimate(flops=int(us * 4e6), bytes_accessed=int(us * 3.0e6), transcendentals=0)


def in_hbm(*arrays):
    return tuple(pltpu.with_memory_space_constraint(a, pltpu.HBM) for a in arrays)


def iota(dim):
    return lax.broadcasted_iota(jnp.int32, (8, 128), dim)


def inside(h_other, h):
    return jnp.where(h_other > 0.0, h_other, h)


def above_z(v):
    t = [pltpu.roll(a, 127, 1) for a in v]
    last = iota(1) == 127
    return [jnp.where(last, t[q + 1], t[q]) if q < Q - 1 else t[q] for q in range(Q)]


def below_z(v):
    t = [pltpu.roll(a, 1, 1) for a in v]
    first = iota(1) == 0
    return [jnp.where(first, t[q - 1], t[q]) if q > 0 else t[q] for q in range(Q)]


def z_coeffs(h):
    up = [a + b for a, b in zip(h, above_z(h))]
    down = [a + b for a, b in zip(h, below_z(h))]
    first, last = iota(1) == 0, iota(1) == 127
    total = [a + b for a, b in zip(up, down)]
    total[0] = up[0] + jnp.where(first, 2.0 * h[0], down[0])
    total[-1] = jnp.where(last, 2.0 * h[-1], up[-1]) + down[-1]
    down[0] = jnp.where(first, 0.0, down[0])
    up[-1] = jnp.where(last, 0.0, up[-1])
    return up, down, total


def add_gram(acc, base, left, right):
    for n, (i, j) in enumerate(PAIRS):
        t = left[i][0] * right[j][0]
        for q in range(1, Q):
            t = t + left[i][q] * right[j][q]
        acc[base + n] += t


def chunk_loop(body):
    def step(i, carry):
        for u in range(UNROLL):
            body(pl.multiple_of(i * (8 * UNROLL), 8) + 8 * u)
        return carry

    lax.fori_loop(0, CHUNKS // UNROLL, step, 0)


def tiles_of(ref, index, row):
    return [ref[(*index, q, pl.ds(row, 8), slice(None))] for q in range(Q)]


def add_spike(ref, index, row, current):
    tile = ref[(*index, slice(0, 128))]
    ref[(*index, slice(0, 128))] = tile + jnp.where(
        (iota(0) == row) & (iota(1) == 0), current, 0.0
    )


def local_cell(elec, f):
    total_y = NY * lax.axis_size("gy")
    cell = elec[f]
    lx = cell // total_y - lax.axis_index("gx") * NX
    ly = cell % total_y - lax.axis_index("gy") * NY
    return lx, ly, (lx >= 0) & (lx < NX) & (ly >= 0) & (ly < NY)


def pack_kernel(
    current, adj, sigma, elec_in, l1_out, g0_out, g1_out, own_out, plane, tiles, far_rows, elec, sems, esem
):
    par = lax.axis_index("gx") % 2
    ypar = lax.axis_index("gy") % 2
    edge = par * (NX - 1)
    ecopy = pltpu.make_async_copy(elec_in, elec, esem)
    ecopy.start()
    copies = []
    for f in range(F + 1):
        src = adj.at[f] if f < F else sigma
        copies.append(pltpu.make_async_copy(src.at[edge], plane.at[f], sems.at[0, f]))
        for side, y in ((0, 0), (1, NY - 8)):
            copies.append(
                pltpu.make_async_copy(
                    src.at[:, pl.ds(y, 8), :], tiles.at[f, side], sems.at[1 + side, f]
                )
            )
    for c in copies:
        c.start()
    ecopy.wait()
    for c in copies:
        c.wait()
    for f in range(F):
        lx, ly, here = local_cell(elec, f)

        @pl.when(here & (lx == edge))
        def _(f=f, ly=ly):
            r8 = pl.multiple_of((ly // 8) * 8, 8)
            add_spike(plane, (f, pl.ds(r8, 8)), ly - r8, current)

        @pl.when(here & (ly < 8))
        def _(f=f, lx=lx, ly=ly):
            add_spike(tiles, (f, 0, lx, slice(0, 8)), ly, current)

        @pl.when(here & (ly >= NY - 8))
        def _(f=f, lx=lx, ly=ly):
            add_spike(tiles, (f, 1, lx, slice(0, 8)), ly - (NY - 8), current)

    for f in range(F + 1):
        k = 1.0 if f < F else 0.5
        for q in range(Q):
            s = slice(q * 128, q * 128 + 128)
            a = (f * Q + q) * NY
            l1_out[a : a + NY, :] = k * plane[f, :, s]
            for x in range(NX):
                a = (f * Q + q) * 8 + x
                for side, (near, far) in enumerate(((0, 1), (7, 6))):
                    own_out[side, a : a + 1, :] = k * tiles[f, side, x, near : near + 1, s]
                    far_rows[side, a : a + 1, :] = k * tiles[f, side, x, far : far + 1, s]
    for f in range(F + 1):
        for q in range(Q):
            t = slice((f * Q + q) * 8, (f * Q + q) * 8 + 8)
            lo, hi = own_out[0, t, :], own_out[1, t, :]
            g0_out[t, :] = jnp.where(ypar == 0, hi, lo)
            g1_out[t, :] = jnp.where(ypar == 0, lo, hi)
            if f < F:
                ht = slice((F * Q + q) * 8, (F * Q + q) * 8 + 8)
                lo = (own_out[0, ht, :] + far_rows[0, ht, :]) * (lo - far_rows[0, t, :])
                hi = (own_out[1, ht, :] + far_rows[1, ht, :]) * (hi - far_rows[1, t, :])
                d = slice(TILE_ROWS + (f * Q + q) * 8, TILE_ROWS + (f * Q + q) * 8 + 8)
                g0_out[d, :] = jnp.where(ypar == 0, hi, lo)
                g1_out[d, :] = jnp.where(ypar == 0, lo, hi)


def pack(current, adj, sigma, electrodes):
    return pl.pallas_call(
        functools.partial(pack_kernel, current),
        out_shape=(
            f32(L1_ROWS, 128),
            f32(G_ROWS, 128),
            f32(G_ROWS, 128),
            f32(2, TILE_ROWS, 128),
        ),
        in_specs=[HBM] * 3,
        out_specs=(VM,) * 4,
        scratch_shapes=[
            pltpu.VMEM((F + 1, NY, NZ), jnp.float32),
            pltpu.VMEM((F + 1, 2, NX, 8, NZ), jnp.float32),
            pltpu.VMEM((2, TILE_ROWS, 128), jnp.float32),
            pltpu.SMEM((F,), jnp.int32),
            pltpu.SemaphoreType.DMA((3, F + 1)),
            pltpu.SemaphoreType.DMA,
        ],
        compiler_params=params(),
        cost_estimate=cost(2),
        name="pack",
    )(*in_hbm(adj, sigma, electrodes))


def load_kernel(current, adj, sigma, elec_in, b_out, h_out, acc, elec, esem):
    ecopy = pltpu.make_async_copy(elec_in, elec, esem)
    ecopy.start()
    acc[...] = jnp.zeros(acc.shape, jnp.float32)

    def place(x, carry):
        for q in range(Q):
            s = slice(q * 128, q * 128 + 128)
            for f in range(F):
                b_out[f, x, q, TOP : TOP + NY, :] = adj[f, x, :, s]
            h_out[x + 1, q, TOP : TOP + NY, :] = 0.5 * sigma[x, :, s]
        return carry

    lax.fori_loop(0, NX, place, 0)
    ecopy.wait()
    for f in range(F):
        lx, ly, here = local_cell(elec, f)

        @pl.when(here)
        def _(f=f, lx=lx, ly=ly):
            r8 = pl.multiple_of((ly // 8) * 8, 8)
            add_spike(b_out, (f, lx, 0, pl.ds(r8 + TOP, 8)), ly - r8, current)

    def plane(x, carry):
        def chunk(r):
            vs = [tiles_of(b_out, (f, x), r + TOP) for f in range(F)]
            add_gram(acc, 0, vs, vs)

        chunk_loop(chunk)
        return carry

    lax.fori_loop(0, NX, plane, 0)


def load_fields(current, adj, sigma, electrodes):
    return pl.pallas_call(
        functools.partial(load_kernel, current),
        out_shape=(f32(F, NX, Q, ROWS, 128), f32(NX + 2, Q, ROWS, 128), f32(10, 8, 128)),
        in_specs=[VM, VM, HBM],
        out_specs=(VM,) * 3,
        scratch_shapes=[pltpu.SMEM((F,), jnp.int32), pltpu.SemaphoreType.DMA],
        compiler_params=params(),
        cost_estimate=cost(2),
        name="load",
    )(adj, sigma, *in_hbm(electrodes))


def chunk_coeffs(h, k, r, x_steps=(-1, 1)):
    at = r + TOP
    own = tiles_of(h, (k,), at)
    up, down, total = z_coeffs(own)
    faces = [(None, up), (None, down)]
    others = [((0, 1), tiles_of(h, (k,), at + 1)), ((0, -1), tiles_of(h, (k,), at - 1))]
    others += [((s, 0), tiles_of(h, (k + s,), at)) for s in x_steps]
    for step, other in others:
        c = [a + b for a, b in zip(own, other)]
        total = [a + b for a, b in zip(total, c)]
        faces.append((step, c))
    return total, faces


def chunk_apply(coeffs, v, f, k, r):
    total, faces = coeffs
    at = r + TOP
    own = tiles_of(v, (f, k), at)
    out = []
    up, down = above_z(own), below_z(own)
    for q in range(Q):
        t = total[q] * own[q] - faces[0][1][q] * up[q] - faces[1][1][q] * down[q]
        u = None
        for s, c in faces[2:]:
            n = c[q] * v[f, k + s[0], q, pl.ds(at + s[1], 8), :]
            u = n if u is None else u + n
        out.append(t - u)
    return own, out


def side_planes(par):
    far = par * (NX - 1)
    near = (NX - 1) - far
    return far, near, par * (NX + 1), (1 - par) * (NX + 1)


def halo_select(ypar, r0, r1, item):
    a = r0[item * 8 : item * 8 + 8, :]
    b = r1[item * 8 : item * 8 + 8, :]
    return jnp.where(ypar == 0, b, a), jnp.where(ypar == 0, a, b)


def edge_plane(b, h, y, x, step):
    def chunk(r):
        coeffs = chunk_coeffs(h, x + 1, r, (step,))
        for f in range(F):
            _, out = chunk_apply(coeffs, b, f, x, r)
            for q in range(Q):
                y[f, x + 1, q, pl.ds(r + TOP, 8), :] = out[q]

    chunk_loop(chunk)


def put_image(y, g, out, base, x):
    for item in range(F * Q):
        f, q = divmod(item, Q)
        a = base + item * NY
        out[a : a + NY, :] = y[f, x + 1, q, TOP : TOP + NY, :]
    base = base + F * PLANE
    out[base : base + 2 * CORNER, :] = jnp.zeros((2 * CORNER, 128), jnp.float32)
    for side in range(2):
        for item in range((F + 1) * Q):
            a = base + side * CORNER + item
            out[a : a + 1, :] = g[side, pl.ds(item * 8 + x, 1), :]


def far_edge_kernel(b_in, h_in, own, r0, r1, b, h, y, g, out, clamped):
    del b_in, h_in
    par = lax.axis_index("gx") % 2
    ypar = lax.axis_index("gy") % 2
    for item in range((F + 1) * Q):
        f, q = divmod(item, Q)
        for side, t in enumerate(halo_select(ypar, r0, r1, item)):
            row = TOP - 1 if side == 0 else TOP + NY
            g[side, item * 8 : item * 8 + 8, :] = t
            if f < F:
                for x in range(NX):
                    b[f, x, q, row : row + 1, :] = g[side, item * 8 + x : item * 8 + x + 1, :]
            else:
                clamped[side, q] = inside(t, own[side, item * 8 : item * 8 + 8, :])
                for x in range(NX):
                    h[x + 1, q, row : row + 1, :] = clamped[side, q, x : x + 1, :]
    far = side_planes(par)[0]
    edge_plane(b, h, y, far, 1 - 2 * par)
    put_image(y, g, out, 0, far)


def near_edge_kernel(b, h_in, y_in, g, rl1, h, y, out):
    del h_in, y_in
    par = lax.axis_index("gx") % 2
    far, near, far_halo, _ = side_planes(par)
    edge_plane(b, h, y, near, 2 * par - 1)
    for q in range(Q):
        for f in range(F):
            a = (f * Q + q) * NY
            out[a : a + NY, :] = b[f, near, q, TOP : TOP + NY, :]
        a = (F * Q + q) * NY
        out[a : a + NY, :] = h[near + 1, q, TOP : TOP + NY, :]
    put_image(y, g, out, L1_ROWS, near)
    border(b, h, y, rl1, far, far_halo)


def border(b, h, y, first, x, halo):
    def chunk(r):
        for q in range(Q):
            own = h[x + 1, q, pl.ds(r + TOP, 8), :]
            beyond = inside(first[pl.ds((F * Q + q) * NY + r, 8), :], own)
            h[halo, q, pl.ds(r + TOP, 8), :] = beyond
            c = own + beyond
            for f in range(F):
                v = b[f, x, q, pl.ds(r + TOP, 8), :]
                flux = c * (v - first[pl.ds((f * Q + q) * NY + r, 8), :])
                at = (f, x + 1, q, pl.ds(r + TOP, 8), slice(None))
                y[at] = y[at] + flux

    chunk_loop(chunk)


def far_edge(b, h, own, r0, r1):
    return pl.pallas_call(
        far_edge_kernel,
        out_shape=(
            f32(F, NX, Q, ROWS, 128),
            f32(NX + 2, Q, ROWS, 128),
            f32(F, NX + 2, Q, ROWS, 128),
            f32(2, TILE_ROWS, 128),
            f32(L2_ROWS, 128),
        ),
        in_specs=[VM] * 5,
        out_specs=(VM,) * 5,
        input_output_aliases={0: 0, 1: 1},
        scratch_shapes=[pltpu.VMEM((2, Q, 8, 128), jnp.float32)],
        compiler_params=params(),
        cost_estimate=cost(10),
        name="far_edge",
    )(b, h, own, r0, r1)


def near_edge(b, h, y, g, rl1):
    return pl.pallas_call(
        near_edge_kernel,
        out_shape=(
            f32(NX + 2, Q, ROWS, 128),
            f32(F, NX + 2, Q, ROWS, 128),
            f32(IN_ROWS, 128),
        ),
        in_specs=[VM] * 5,
        out_specs=(VM,) * 3,
        input_output_aliases={1: 0, 2: 1},
        compiler_params=params(),
        cost_estimate=cost(20),
        name="near_edge",
    )(b, h, y, g, rl1)


def row_halo(own, rh, side, y, tmp):
    count = lax.axis_size("gy")
    ay = lax.axis_index("gy")
    valid = ay > 0 if side == 0 else ay < count - 1
    row = TOP - 1 if side == 0 else TOP + NY
    sub = iota(0)
    own_at = lambda f, q: own[side, (f * Q + q) * 8 : (f * Q + q) * 8 + 8, :]
    h_r = [rh(F * Q + q) for q in range(Q)]
    zu, zd, total = z_coeffs(h_r)
    across = [h_r[q] + own_at(F, q) for q in range(Q)]
    up = [jnp.where(sub == NX - 1, 0.0, a + pltpu.roll(a, 7, 0)) for a in h_r]
    down = [jnp.where(sub == 0, 0.0, a + pltpu.roll(a, 1, 0)) for a in h_r]
    total = [sum(t) for t in zip(total, across, up, down)]
    for f in range(F):
        v = [rh(f * Q + q) for q in range(Q)]
        zp, zm = above_z(v), below_z(v)
        for q in range(Q):
            out = total[q] * v[q] + rh((F + 1 + f) * Q + q) - across[q] * own_at(f, q)
            out = out - up[q] * pltpu.roll(v[q], 7, 0) - down[q] * pltpu.roll(v[q], 1, 0)
            out = out - zu[q] * zp[q] - zd[q] * zm[q]
            tmp[side, f, q] = jnp.where(valid, out, 0.0)
            for x in range(NX):
                y[f, x + 1, q, row : row + 1, :] = tmp[side, f, q, x : x + 1, :]


def z_plane(h, y, d, acc, x):
    def chunk(r):
        coeffs = chunk_coeffs(h, x + 1, r)
        for f in range(F):
            v, out = chunk_apply(coeffs, y, f, x + 1, r)
            for q in range(Q):
                d[f, x, q, pl.ds(r, 8), :] = out[q] - v[q]

    def grams(r):
        ys = [tiles_of(y, (f, x + 1), r + TOP) for f in range(F)]
        add_gram(acc, 20, ys, [tiles_of(d, (f, x), r) for f in range(F)])

    chunk_loop(chunk)
    chunk_loop(grams)


def plane_grams(b, y, acc, x):
    def chunk(r):
        vs = [tiles_of(b, (f, x), r + TOP) for f in range(F)]
        outs = [tiles_of(y, (f, x + 1), r + TOP) for f in range(F)]
        add_gram(acc, 0, vs, outs)
        add_gram(acc, 10, outs, outs)

    chunk_loop(chunk)


def inner_kernel(b, h, own, r0, r1, y_in, y, z, acc, tmp):
    del y_in
    par = lax.axis_index("gx") % 2
    ypar = lax.axis_index("gy") % 2
    far = side_planes(par)[0]
    acc[...] = jnp.zeros(acc.shape, jnp.float32)
    for side in range(2):
        row_halo(own, lambda item: halo_select(ypar, r0, r1, item)[side], side, y, tmp)

    def y_plane(x, carry):
        def chunk(r):
            coeffs = chunk_coeffs(h, x + 1, r)
            for f in range(F):
                _, out = chunk_apply(coeffs, b, f, x, r)
                for q in range(Q):
                    y[f, x + 1, q, pl.ds(r + TOP, 8), :] = out[q]

        chunk_loop(chunk)
        plane_grams(b, y, acc, x)
        return carry

    lax.fori_loop(1, NX - 1, y_plane, 0)
    plane_grams(b, y, acc, far)

    def z_loop(n, carry):
        z_plane(h, y, z, acc, jnp.where(par == 0, n, NX - 1 - n))
        return carry

    lax.fori_loop(1, NX - 2, z_loop, 0)


def inner(b, h, own, r0, r1, y):
    return pl.pallas_call(
        inner_kernel,
        out_shape=(
            f32(F, NX + 2, Q, ROWS, 128),
            f32(F, NX, Q, NY, 128),
            f32(30, 8, 128),
        ),
        in_specs=[VM] * 6,
        out_specs=(VM,) * 3,
        input_output_aliases={5: 0},
        scratch_shapes=[pltpu.VMEM((2, F, Q, 8, 128), jnp.float32)],
        compiler_params=params(),
        cost_estimate=cost(0),
        name="inner",
    )(b, h, own, r0, r1, y)


def halo_image(b, h, y, first, second, s0, x, halo):
    count_x, count_y = lax.axis_size("gx"), lax.axis_size("gy")
    ax, ay = lax.axis_index("gx"), lax.axis_index("gy")
    valid = jnp.where(x == 0, ax > 0, ax < count_x - 1)

    def chunk(r):
        for q in range(Q):
            c = h[x + 1, q, pl.ds(r + TOP, 8), :] + h[halo, q, pl.ds(r + TOP, 8), :]
            for f in range(F):
                a = (f * Q + q) * NY + r
                flux = c * (b[f, x, q, pl.ds(r + TOP, 8), :] - first[pl.ds(a, 8), :])
                other = second[pl.ds(s0 + a, 8), :] - flux
                y[f, halo, q, pl.ds(r + TOP, 8), :] = jnp.where(valid, other, 0.0)

    chunk_loop(chunk)
    for side in range(2):
        row = TOP - 1 if side == 0 else TOP + NY
        valid_row = ay > 0 if side == 0 else ay < count_y - 1
        base = s0 + F * PLANE + side * CORNER
        for q in range(Q):
            h_r = h[x + 1, q, row : row + 1, :]
            a = base + F * Q + q
            c = h_r + inside(second[a : a + 1, :], h_r)
            for f in range(F):
                v = b[f, x, q, row : row + 1, :]
                a = base + f * Q + q
                flux = jnp.where(valid_row, c * (v - second[a : a + 1, :]), 0.0)
                y[f, x + 1, q, row : row + 1, :] = y[f, x + 1, q, row : row + 1, :] + flux


def near_kernel(b, h_in, rin, y_in, z_in, acc_in, h, y, z, acc):
    del h_in, y_in, z_in
    par = lax.axis_index("gx") % 2
    _, near, _, halo = side_planes(par)
    acc[...] = acc_in[...]
    border(b, h, y, rin, near, halo)
    halo_image(b, h, y, rin, rin, L1_ROWS, near, halo)
    plane_grams(b, y, acc, near)

    def z_loop(n, carry):
        z_plane(h, y, z, acc, jnp.where(par == 0, n, NX - 1 - n))
        return carry

    lax.fori_loop(NX - 2, NX, z_loop, 0)


def near_side(b, h, rin, y, z, acc):
    return pl.pallas_call(
        near_kernel,
        out_shape=(
            f32(NX + 2, Q, ROWS, 128),
            f32(F, NX + 2, Q, ROWS, 128),
            f32(F, NX, Q, NY, 128),
            f32(30, 8, 128),
        ),
        in_specs=[VM] * 6,
        out_specs=(VM,) * 4,
        input_output_aliases={1: 0, 3: 1, 4: 2},
        compiler_params=params(),
        cost_estimate=cost(0),
        name="near",
    )(b, h, rin, y, z, acc)


def far_kernel(b, h, rl1, rl2, y_in, z_in, accb, acc_in, y, z, msg, acc):
    del y_in, z_in
    par = lax.axis_index("gx") % 2
    far, _, halo, _ = side_planes(par)
    acc[...] = acc_in[...]
    halo_image(b, h, y, rl1, rl2, 0, far, halo)
    z_plane(h, y, z, acc, far)
    sums = jnp.concatenate(
        [jnp.sum(accb[k], axis=0, keepdims=True) for k in range(10)]
        + [jnp.sum(acc[k], axis=0, keepdims=True) for k in range(30)]
        + [jnp.zeros((88, 128), jnp.float32)],
        axis=0,
    )
    msg[...] = lax.dot_general(
        jnp.ones((8, 128), jnp.float32),
        sums,
        (((1,), (1,)), ((), ())),
        precision=lax.Precision.HIGHEST,
        preferred_element_type=jnp.float32,
    )


def far_side(b, h, rl1, rl2, y, z, accb, acc):
    return pl.pallas_call(
        far_kernel,
        out_shape=(f32(F, NX + 2, Q, ROWS, 128), f32(F, NX, Q, NY, 128), f32(8, 128)),
        in_specs=[VM] * 8,
        out_specs=(VM,) * 3,
        input_output_aliases={4: 0, 5: 1},
        scratch_shapes=[pltpu.VMEM((30, 8, 128), jnp.float32)],
        compiler_params=params(),
        cost_estimate=cost(3),
        name="far",
    )(b, h, rl1, rl2, y, z, accb, acc)


def mm(a, b, ta=False):
    at = (lambda i, k: a[k][i]) if ta else (lambda i, k: a[i][k])
    return [
        [sum((at(i, k) * b[k][j] for k in range(1, F)), at(i, 0) * b[0][j]) for j in range(F)]
        for i in range(F)
    ]


def add(a, b, s=1.0):
    return [[a[i][j] + s * b[i][j] for j in range(F)] for i in range(F)]


def symmetric(a):
    return [[a[i][j] if i == j else 0.5 * (a[i][j] + a[j][i]) for j in range(F)] for i in range(F)]


def spd_solve(a, b):
    low = [[None] * F for _ in range(F)]
    d, inv = [None] * F, [None] * F
    for j in range(F):
        t = a[j][j]
        for k in range(j):
            t = t - low[j][k] * low[j][k] * d[k]
        d[j] = t
        inv[j] = 1.0 / t
        for i in range(j + 1, F):
            t = a[i][j]
            for k in range(j):
                t = t - low[i][k] * low[j][k] * d[k]
            low[i][j] = t * inv[j]
    x = [list(row) for row in b]
    for i in range(F):
        for k in range(i):
            for j in range(F):
                x[i][j] = x[i][j] - low[i][k] * x[k][j]
    for i in range(F):
        x[i] = [e * inv[i] for e in x[i]]
    for i in reversed(range(F)):
        for k in range(i + 1, F):
            for j in range(F):
                x[i][j] = x[i][j] - low[k][i] * x[k][j]
    return x


def step_matrices(entry):
    grams = []
    for g in range(4):
        m = [[None] * F for _ in range(F)]
        for n, (i, j) in enumerate(PAIRS):
            m[i][j] = m[j][i] = entry(10 * g + n)
        grams.append(m)
    bb, by, yy, yd = grams
    yz = add(yd, yy)
    alpha = spd_solve(by, bb)
    new = symmetric(add(mm(alpha, mm(yy, alpha), ta=True), bb, -1.0))
    beta = spd_solve(bb, new)
    e = [[beta[i][j] + 1.0 if i == j else beta[i][j] for j in range(F)] for i in range(F)]
    cross = mm(e, mm(yy, alpha), ta=True)
    curv = add(mm(e, mm(by, e), ta=True), mm(alpha, mm(yz, alpha), ta=True))
    curv = [[curv[i][j] - cross[i][j] - cross[j][i] for j in range(F)] for i in range(F)]
    alpha2 = spd_solve(symmetric(curv), new)
    m1 = add(alpha, mm(e, alpha2))
    m2 = mm(alpha, alpha2)
    return m1, m2


def final_kernel(w, b, y, d, xs_hbm, res_hbm, coef, xs_out, res_out, sems):
    total = jnp.sum(w[...], axis=0, keepdims=True)
    sub = lax.broadcasted_iota(jnp.int32, (128, 128), 0)
    lane = lax.broadcasted_iota(jnp.int32, (128, 128), 1)
    spread = lax.dot_general(
        jnp.where(sub == lane, total, 0.0),
        jnp.ones((128, 128), jnp.float32),
        (((1,), (0,)), ((), ())),
        precision=lax.Precision.HIGHEST,
        preferred_element_type=jnp.float32,
    )
    m1, m2 = step_matrices(lambda k: spread[k : k + 1, :])
    for i in range(F):
        for j in range(F):
            n = i * F + j
            coef[n] = jnp.broadcast_to(m1[i][j], (8, 128))
            coef[16 + n] = jnp.broadcast_to(m2[i][j], (8, 128))
            coef[32 + n] = jnp.broadcast_to(m1[i][j] - m2[i][j], (8, 128))

    def copies(x):
        return (
            pltpu.make_async_copy(xs_out.at[:, x], xs_hbm.at[:, x], sems.at[0, x]),
            pltpu.make_async_copy(res_out.at[:, x], res_hbm.at[:, x], sems.at[1, x]),
        )

    def plane(x, carry):
        def body(i, inner):
            r = pl.multiple_of(i * 8, 8)
            for q in range(Q):
                bs = [b[f, x, q, pl.ds(r + TOP, 8), :] for f in range(F)]
                ys = [y[f, x + 1, q, pl.ds(r + TOP, 8), :] for f in range(F)]
                ds = [d[f, x, q, pl.ds(r, 8), :] for f in range(F)]
                es = [bs[f] - ys[f] for f in range(F)]
                for j in range(F):
                    p = ys[0] * coef[32 + j]
                    for k in range(1, F):
                        p = p + ys[k] * coef[32 + k * F + j]
                    ro = bs[j] - p
                    for k in range(F):
                        p = p + es[k] * coef[k * F + j]
                        ro = ro + ds[k] * coef[16 + k * F + j]
                    s = slice(q * 128, q * 128 + 128)
                    xs_out[j, x, pl.ds(r, 8), s] = p
                    res_out[j, x, pl.ds(r, 8), s] = ro
            return inner

        lax.fori_loop(0, CHUNKS, body, 0)
        for c in copies(x):
            c.start()
        return carry

    lax.fori_loop(0, NX, plane, 0)
    for x in range(NX):
        for c in copies(x):
            c.wait()


def final(w, b, y, d):
    out = jax.ShapeDtypeStruct((F, NX, NY, NZ), jnp.float32)
    return pl.pallas_call(
        final_kernel,
        out_shape=(out, out),
        in_specs=[VM] * 4,
        out_specs=(HBM, HBM),
        scratch_shapes=[
            pltpu.VMEM((48, 8, 128), jnp.float32),
            pltpu.VMEM((F, NX, NY, NZ), jnp.float32),
            pltpu.VMEM((F, NX, NY, NZ), jnp.float32),
            pltpu.SemaphoreType.DMA((2, NX)),
        ],
        compiler_params=params(),
        cost_estimate=cost(5),
        name="final",
    )(w, b, y, d)


def exchange(x, sizes, partner):
    nx, ny = sizes
    pairs = []
    for a in range(nx):
        for c in range(ny):
            ta, tc = partner(a, c)
            if 0 <= ta < nx and 0 <= tc < ny:
                pairs.append((a * ny + c, ta * ny + tc))
    return lax.ppermute(x, AXES, pairs)


def shards(sizes, adjoint_source, conductivity, electrodes):
    nx, ny = sizes
    current = math.sqrt(nx * NX * ny * NY * NZ)
    border_pair = lambda a, c: (a + 1 if a % 2 else a - 1, c)
    inputs = (current, adjoint_source, conductivity, electrodes)
    l1, g0, g1, own = pack(*inputs)
    rl1 = exchange(l1, sizes, border_pair)
    r0 = exchange(g0, sizes, lambda a, c: (a, c ^ 1))
    r1 = exchange(g1, sizes, lambda a, c: (a, c + 1 if c % 2 else c - 1))
    b, h, accb = load_fields(*inputs)
    b, h, y, g, l2 = far_edge(b, h, own, r0, r1)
    rl2 = exchange(l2, sizes, border_pair)
    h, y, core = near_edge(b, h, y, g, rl1)
    rin = exchange(core, sizes, lambda a, c: (a ^ 1, c))
    y, z, acc = inner(b, h, own, r0, r1, y)
    h, y, z, acc = near_side(b, h, rin, y, z, acc)
    y, z, msg = far_side(b, h, rl1, rl2, y, z, accb, acc)
    sent = jnp.broadcast_to(msg[0:1][None], (nx * ny, 1, 128))
    w = lax.all_to_all(sent, AXES, 0, 0).reshape(nx * ny, 128)
    return final(w, b, y, z)


def solution(mesh):
    sizes = (mesh.shape["gx"], mesh.shape["gy"])
    placed = (P(None, "gx", "gy", None), P("gx", "gy", None), P())
    return jax.shard_map(
        functools.partial(shards, sizes),
        mesh=mesh,
        in_specs=placed,
        out_specs=(P(None, "gx", "gy", None), P(None, "gx", "gy", None)),
        check_vma=False,
    )
```

```python
import functools
import math

import jax
import jax.numpy as jnp
from jax import lax
from jax.experimental import pallas as pl
from jax.experimental.pallas import tpu as pltpu
from jax.sharding import PartitionSpec as P

AXES = ("gx", "gy")
F = 4
NX = 8
NY = 64
NZ = 512
Q = NZ // 128
CHUNKS = NY // 8
UNROLL = 4
PAIRS = [(i, j) for i in range(F) for j in range(i, F)]
TOP = 8
ROWS = NY + 2 * TOP
PLANE = Q * NY
L1_ROWS = (F + 1) * PLANE
CORNER = 24
L2_ROWS = F * PLANE + 2 * CORNER
IN_ROWS = L1_ROWS + L2_ROWS
TILE_ROWS = (F + 1) * Q * 8
G_ROWS = TILE_ROWS + F * Q * 8
VMEM_LIMIT = 16 * 1024 * 1024

VM = pl.BlockSpec(memory_space=pltpu.VMEM)
HBM = pl.BlockSpec(memory_space=pltpu.HBM)


def f32(*shape):
    return pltpu.VMEM(shape, jnp.float32)


def params():
    return pltpu.CompilerParams(vmem_limit_bytes=VMEM_LIMIT)


def cost(us):
    return pl.CostEstimate(flops=int(us * 4e6), bytes_accessed=int(us * 3.0e6), transcendentals=0)


def in_hbm(*arrays):
    return tuple(pltpu.with_memory_space_constraint(a, pltpu.HBM) for a in arrays)


def iota(dim):
    return lax.broadcasted_iota(jnp.int32, (8, 128), dim)


def inside(h_other, h):
    return jnp.where(h_other > 0.0, h_other, h)


def above_z(v):
    t = [pltpu.roll(a, 127, 1) for a in v]
    last = iota(1) == 127
    return [jnp.where(last, t[q + 1], t[q]) if q < Q - 1 else t[q] for q in range(Q)]


def below_z(v):
    t = [pltpu.roll(a, 1, 1) for a in v]
    first = iota(1) == 0
    return [jnp.where(first, t[q - 1], t[q]) if q > 0 else t[q] for q in range(Q)]


def z_coeffs(h):
    up = [a + b for a, b in zip(h, above_z(h))]
    down = [a + b for a, b in zip(h, below_z(h))]
    first, last = iota(1) == 0, iota(1) == 127
    total = [a + b for a, b in zip(up, down)]
    total[0] = up[0] + jnp.where(first, 2.0 * h[0], down[0])
    total[-1] = jnp.where(last, 2.0 * h[-1], up[-1]) + down[-1]
    down[0] = jnp.where(first, 0.0, down[0])
    up[-1] = jnp.where(last, 0.0, up[-1])
    return up, down, total


def add_gram(acc, base, left, right):
    for n, (i, j) in enumerate(PAIRS):
        t = left[i][0] * right[j][0]
        for q in range(1, Q):
            t = t + left[i][q] * right[j][q]
        acc[base + n] += t


def chunk_loop(body):
    def step(i, carry):
        for u in range(UNROLL):
            body(pl.multiple_of(i * (8 * UNROLL), 8) + 8 * u)
        return carry

    lax.fori_loop(0, CHUNKS // UNROLL, step, 0)


def tiles_of(ref, index, row):
    return [ref[(*index, q, pl.ds(row, 8), slice(None))] for q in range(Q)]


def add_spike(ref, index, row, current):
    tile = ref[(*index, slice(0, 128))]
    ref[(*index, slice(0, 128))] = tile + jnp.where(
        (iota(0) == row) & (iota(1) == 0), current, 0.0
    )


def local_cell(elec, f):
    total_y = NY * lax.axis_size("gy")
    cell = elec[f]
    lx = cell // total_y - lax.axis_index("gx") * NX
    ly = cell % total_y - lax.axis_index("gy") * NY
    return lx, ly, (lx >= 0) & (lx < NX) & (ly >= 0) & (ly < NY)


def pack_kernel(
    current, adj, sigma, elec_in, l1_out, g0_out, g1_out, own_out, plane, tiles, far_rows, elec, sems, esem
):
    par = lax.axis_index("gx") % 2
    ypar = lax.axis_index("gy") % 2
    edge = par * (NX - 1)
    ecopy = pltpu.make_async_copy(elec_in, elec, esem)
    ecopy.start()
    copies = []
    for f in range(F + 1):
        src = adj.at[f] if f < F else sigma
        copies.append(pltpu.make_async_copy(src.at[edge], plane.at[f], sems.at[0, f]))
        for side, y in ((0, 0), (1, NY - 8)):
            copies.append(
                pltpu.make_async_copy(
                    src.at[:, pl.ds(y, 8), :], tiles.at[f, side], sems.at[1 + side, f]
                )
            )
    for c in copies:
        c.start()
    ecopy.wait()
    for c in copies:
        c.wait()
    for f in range(F):
        lx, ly, here = local_cell(elec, f)

        @pl.when(here & (lx == edge))
        def _(f=f, ly=ly):
            r8 = pl.multiple_of((ly // 8) * 8, 8)
            add_spike(plane, (f, pl.ds(r8, 8)), ly - r8, current)

        @pl.when(here & (ly < 8))
        def _(f=f, lx=lx, ly=ly):
            add_spike(tiles, (f, 0, lx, slice(0, 8)), ly, current)

        @pl.when(here & (ly >= NY - 8))
        def _(f=f, lx=lx, ly=ly):
            add_spike(tiles, (f, 1, lx, slice(0, 8)), ly - (NY - 8), current)

    for f in range(F + 1):
        k = 1.0 if f < F else 0.5
        for q in range(Q):
            s = slice(q * 128, q * 128 + 128)
            a = (f * Q + q) * NY
            l1_out[a : a + NY, :] = k * plane[f, :, s]
            for x in range(NX):
                a = (f * Q + q) * 8 + x
                for side, (near, far) in enumerate(((0, 1), (7, 6))):
                    own_out[side, a : a + 1, :] = k * tiles[f, side, x, near : near + 1, s]
                    far_rows[side, a : a + 1, :] = k * tiles[f, side, x, far : far + 1, s]
    for f in range(F + 1):
        for q in range(Q):
            t = slice((f * Q + q) * 8, (f * Q + q) * 8 + 8)
            lo, hi = own_out[0, t, :], own_out[1, t, :]
            g0_out[t, :] = jnp.where(ypar == 0, hi, lo)
            g1_out[t, :] = jnp.where(ypar == 0, lo, hi)
            if f < F:
                ht = slice((F * Q + q) * 8, (F * Q + q) * 8 + 8)
                lo = (own_out[0, ht, :] + far_rows[0, ht, :]) * (lo - far_rows[0, t, :])
                hi = (own_out[1, ht, :] + far_rows[1, ht, :]) * (hi - far_rows[1, t, :])
                d = slice(TILE_ROWS + (f * Q + q) * 8, TILE_ROWS + (f * Q + q) * 8 + 8)
                g0_out[d, :] = jnp.where(ypar == 0, hi, lo)
                g1_out[d, :] = jnp.where(ypar == 0, lo, hi)


def pack(current, adj, sigma, electrodes):
    return pl.pallas_call(
        functools.partial(pack_kernel, current),
        out_shape=(
            f32(L1_ROWS, 128),
            f32(G_ROWS, 128),
            f32(G_ROWS, 128),
            f32(2, TILE_ROWS, 128),
        ),
        in_specs=[HBM] * 3,
        out_specs=(VM,) * 4,
        scratch_shapes=[
            pltpu.VMEM((F + 1, NY, NZ), jnp.float32),
            pltpu.VMEM((F + 1, 2, NX, 8, NZ), jnp.float32),
            pltpu.VMEM((2, TILE_ROWS, 128), jnp.float32),
            pltpu.SMEM((F,), jnp.int32),
            pltpu.SemaphoreType.DMA((3, F + 1)),
            pltpu.SemaphoreType.DMA,
        ],
        compiler_params=params(),
        cost_estimate=cost(2),
        name="pack",
    )(*in_hbm(adj, sigma, electrodes))


def load_kernel(current, adj, sigma, elec_in, b_out, h_out, y, acc, elec, esem):
    ecopy = pltpu.make_async_copy(elec_in, elec, esem)
    ecopy.start()
    acc[...] = jnp.zeros(acc.shape, jnp.float32)

    def place(x, carry):
        for q in range(Q):
            s = slice(q * 128, q * 128 + 128)
            for f in range(F):
                b_out[f, x, q, TOP : TOP + NY, :] = adj[f, x, :, s]
            h_out[x + 1, q, TOP : TOP + NY, :] = 0.5 * sigma[x, :, s]
            for row, edge in ((TOP - 1, TOP), (TOP + NY, TOP + NY - 1)):
                h_out[x + 1, q, row : row + 1, :] = -h_out[x + 1, q, edge : edge + 1, :]
                for f in range(F):
                    b_out[f, x, q, row : row + 1, :] = jnp.zeros((1, 128), jnp.float32)
        return carry

    lax.fori_loop(0, NX, place, 0)
    ecopy.wait()
    for f in range(F):
        lx, ly, here = local_cell(elec, f)

        @pl.when(here)
        def _(f=f, lx=lx, ly=ly):
            r8 = pl.multiple_of((ly // 8) * 8, 8)
            add_spike(b_out, (f, lx, 0, pl.ds(r8 + TOP, 8)), ly - r8, current)

    def plane(x, carry):
        def chunk(r):
            vs = [tiles_of(b_out, (f, x), r + TOP) for f in range(F)]
            add_gram(acc, 0, vs, vs)

        chunk_loop(chunk)
        return carry

    lax.fori_loop(0, NX, plane, 0)

    def image(x, carry):
        def chunk(r):
            coeffs = chunk_coeffs(h_out, x + 1, r)
            for f in range(F):
                _, out = chunk_apply(coeffs, b_out, f, x, r)
                for q in range(Q):
                    y[f, x + 1, q, pl.ds(r + TOP, 8), :] = out[q]

        chunk_loop(chunk)
        return carry

    lax.fori_loop(1, NX - 1, image, 0)


def load_fields(current, adj, sigma, electrodes):
    return pl.pallas_call(
        functools.partial(load_kernel, current),
        out_shape=(
            f32(F, NX, Q, ROWS, 128),
            f32(NX + 2, Q, ROWS, 128),
            f32(F, NX + 2, Q, ROWS, 128),
            f32(10, 8, 128),
        ),
        in_specs=[VM, VM, HBM],
        out_specs=(VM,) * 4,
        scratch_shapes=[pltpu.SMEM((F,), jnp.int32), pltpu.SemaphoreType.DMA],
        compiler_params=params(),
        cost_estimate=cost(2),
        name="load",
    )(adj, sigma, *in_hbm(electrodes))


def chunk_coeffs(h, k, r, x_steps=(-1, 1)):
    at = r + TOP
    own = tiles_of(h, (k,), at)
    up, down, total = z_coeffs(own)
    faces = [(None, up), (None, down)]
    others = [((0, 1), tiles_of(h, (k,), at + 1)), ((0, -1), tiles_of(h, (k,), at - 1))]
    others += [((s, 0), tiles_of(h, (k + s,), at)) for s in x_steps]
    for step, other in others:
        c = [a + b for a, b in zip(own, other)]
        total = [a + b for a, b in zip(total, c)]
        faces.append((step, c))
    return total, faces


def chunk_apply(coeffs, v, f, k, r):
    total, faces = coeffs
    at = r + TOP
    own = tiles_of(v, (f, k), at)
    out = []
    up, down = above_z(own), below_z(own)
    for q in range(Q):
        t = total[q] * own[q] - faces[0][1][q] * up[q] - faces[1][1][q] * down[q]
        u = None
        for s, c in faces[2:]:
            n = c[q] * v[f, k + s[0], q, pl.ds(at + s[1], 8), :]
            u = n if u is None else u + n
        out.append(t - u)
    return own, out


def side_planes(par):
    far = par * (NX - 1)
    near = (NX - 1) - far
    return far, near, par * (NX + 1), (1 - par) * (NX + 1)


def halo_select(ypar, r0, r1, item):
    a = r0[item * 8 : item * 8 + 8, :]
    b = r1[item * 8 : item * 8 + 8, :]
    return jnp.where(ypar == 0, b, a), jnp.where(ypar == 0, a, b)


def edge_plane(b, h, y, x, step):
    def chunk(r):
        coeffs = chunk_coeffs(h, x + 1, r, (step,))
        for f in range(F):
            _, out = chunk_apply(coeffs, b, f, x, r)
            for q in range(Q):
                y[f, x + 1, q, pl.ds(r + TOP, 8), :] = out[q]

    chunk_loop(chunk)


def put_image(y, g, out, base, x):
    for item in range(F * Q):
        f, q = divmod(item, Q)
        a = base + item * NY
        out[a : a + NY, :] = y[f, x + 1, q, TOP : TOP + NY, :]
    base = base + F * PLANE
    out[base : base + 2 * CORNER, :] = jnp.zeros((2 * CORNER, 128), jnp.float32)
    for side in range(2):
        for item in range((F + 1) * Q):
            a = base + side * CORNER + item
            out[a : a + 1, :] = g[side, pl.ds(item * 8 + x, 1), :]


def far_edge_kernel(b_in, h_in, y_in, own, r0, r1, b, h, y, g, out, clamped):
    del b_in, h_in, y_in
    par = lax.axis_index("gx") % 2
    ypar = lax.axis_index("gy") % 2
    for item in range((F + 1) * Q):
        f, q = divmod(item, Q)
        for side, t in enumerate(halo_select(ypar, r0, r1, item)):
            row = TOP - 1 if side == 0 else TOP + NY
            g[side, item * 8 : item * 8 + 8, :] = t
            if f < F:
                for x in range(NX):
                    b[f, x, q, row : row + 1, :] = g[side, item * 8 + x : item * 8 + x + 1, :]
            else:
                clamped[side, q] = inside(t, own[side, item * 8 : item * 8 + 8, :])
                for x in range(NX):
                    h[x + 1, q, row : row + 1, :] = clamped[side, q, x : x + 1, :]
    far = side_planes(par)[0]
    edge_plane(b, h, y, far, 1 - 2 * par)
    put_image(y, g, out, 0, far)


def near_edge_kernel(b, h_in, y_in, g, rl1, h, y, out):
    del h_in, y_in
    par = lax.axis_index("gx") % 2
    far, near, far_halo, _ = side_planes(par)
    edge_plane(b, h, y, near, 2 * par - 1)
    for q in range(Q):
        for f in range(F):
            a = (f * Q + q) * NY
            out[a : a + NY, :] = b[f, near, q, TOP : TOP + NY, :]
        a = (F * Q + q) * NY
        out[a : a + NY, :] = h[near + 1, q, TOP : TOP + NY, :]
    put_image(y, g, out, L1_ROWS, near)
    border(b, h, y, rl1, far, far_halo)


def border(b, h, y, first, x, halo):
    def chunk(r):
        for q in range(Q):
            own = h[x + 1, q, pl.ds(r + TOP, 8), :]
            beyond = inside(first[pl.ds((F * Q + q) * NY + r, 8), :], own)
            h[halo, q, pl.ds(r + TOP, 8), :] = beyond
            c = own + beyond
            for f in range(F):
                v = b[f, x, q, pl.ds(r + TOP, 8), :]
                flux = c * (v - first[pl.ds((f * Q + q) * NY + r, 8), :])
                at = (f, x + 1, q, pl.ds(r + TOP, 8), slice(None))
                y[at] = y[at] + flux

    chunk_loop(chunk)


def far_edge(b, h, y, own, r0, r1):
    return pl.pallas_call(
        far_edge_kernel,
        out_shape=(
            f32(F, NX, Q, ROWS, 128),
            f32(NX + 2, Q, ROWS, 128),
            f32(F, NX + 2, Q, ROWS, 128),
            f32(2, TILE_ROWS, 128),
            f32(L2_ROWS, 128),
        ),
        in_specs=[VM] * 6,
        out_specs=(VM,) * 5,
        input_output_aliases={0: 0, 1: 1, 2: 2},
        scratch_shapes=[pltpu.VMEM((2, Q, 8, 128), jnp.float32)],
        compiler_params=params(),
        cost_estimate=cost(10),
        name="far_edge",
    )(b, h, y, own, r0, r1)


def near_edge(b, h, y, g, rl1):
    return pl.pallas_call(
        near_edge_kernel,
        out_shape=(
            f32(NX + 2, Q, ROWS, 128),
            f32(F, NX + 2, Q, ROWS, 128),
            f32(IN_ROWS, 128),
        ),
        in_specs=[VM] * 5,
        out_specs=(VM,) * 3,
        input_output_aliases={1: 0, 2: 1},
        compiler_params=params(),
        cost_estimate=cost(20),
        name="near_edge",
    )(b, h, y, g, rl1)


def row_halo(own, rh, side, y, tmp):
    count = lax.axis_size("gy")
    ay = lax.axis_index("gy")
    valid = ay > 0 if side == 0 else ay < count - 1
    row = TOP - 1 if side == 0 else TOP + NY
    sub = iota(0)
    own_at = lambda f, q: own[side, (f * Q + q) * 8 : (f * Q + q) * 8 + 8, :]
    h_r = [rh(F * Q + q) for q in range(Q)]
    zu, zd, total = z_coeffs(h_r)
    across = [h_r[q] + own_at(F, q) for q in range(Q)]
    up = [jnp.where(sub == NX - 1, 0.0, a + pltpu.roll(a, 7, 0)) for a in h_r]
    down = [jnp.where(sub == 0, 0.0, a + pltpu.roll(a, 1, 0)) for a in h_r]
    total = [sum(t) for t in zip(total, across, up, down)]
    for f in range(F):
        v = [rh(f * Q + q) for q in range(Q)]
        zp, zm = above_z(v), below_z(v)
        for q in range(Q):
            out = total[q] * v[q] + rh((F + 1 + f) * Q + q) - across[q] * own_at(f, q)
            out = out - up[q] * pltpu.roll(v[q], 7, 0) - down[q] * pltpu.roll(v[q], 1, 0)
            out = out - zu[q] * zp[q] - zd[q] * zm[q]
            tmp[side, f, q] = jnp.where(valid, out, 0.0)
            for x in range(NX):
                y[f, x + 1, q, row : row + 1, :] = tmp[side, f, q, x : x + 1, :]


def halo_rows(own, rh, y, tmp):
    for side in range(2):
        row = TOP if side == 0 else TOP + NY - 1
        for q in range(Q):
            h_own = own[side, (F * Q + q) * 8 : (F * Q + q) * 8 + 8, :]
            c = h_own + inside(rh(F * Q + q)[side], h_own)
            for f in range(F):
                item = f * Q + q
                tmp[2 + side, f, q] = c * (own[side, item * 8 : item * 8 + 8, :] - rh(item)[side])
                for x in range(1, NX - 1):
                    y[f, x + 1, q, row : row + 1, :] += tmp[2 + side, f, q, x : x + 1, :]


def z_plane(h, y, d, acc, x):
    def chunk(r):
        coeffs = chunk_coeffs(h, x + 1, r)
        for f in range(F):
            v, out = chunk_apply(coeffs, y, f, x + 1, r)
            for q in range(Q):
                d[f, x, q, pl.ds(r, 8), :] = out[q] - v[q]

    def grams(r):
        ys = [tiles_of(y, (f, x + 1), r + TOP) for f in range(F)]
        add_gram(acc, 20, ys, [tiles_of(d, (f, x), r) for f in range(F)])

    chunk_loop(chunk)
    chunk_loop(grams)


def plane_grams(b, y, acc, x):
    def chunk(r):
        vs = [tiles_of(b, (f, x), r + TOP) for f in range(F)]
        outs = [tiles_of(y, (f, x + 1), r + TOP) for f in range(F)]
        add_gram(acc, 0, vs, outs)
        add_gram(acc, 10, outs, outs)

    chunk_loop(chunk)


def inner_kernel(b, h, own, r0, r1, y_in, y, z, acc, tmp):
    del y_in
    par = lax.axis_index("gx") % 2
    ypar = lax.axis_index("gy") % 2
    far = side_planes(par)[0]
    acc[...] = jnp.zeros(acc.shape, jnp.float32)
    for side in range(2):
        row_halo(own, lambda item: halo_select(ypar, r0, r1, item)[side], side, y, tmp)

    halo_rows(own, lambda item: halo_select(ypar, r0, r1, item), y, tmp)

    def y_plane(x, carry):
        plane_grams(b, y, acc, x)
        return carry

    lax.fori_loop(1, NX - 1, y_plane, 0)
    plane_grams(b, y, acc, far)

    def z_loop(n, carry):
        z_plane(h, y, z, acc, jnp.where(par == 0, n, NX - 1 - n))
        return carry

    lax.fori_loop(1, NX - 2, z_loop, 0)


def inner(b, h, own, r0, r1, y):
    return pl.pallas_call(
        inner_kernel,
        out_shape=(
            f32(F, NX + 2, Q, ROWS, 128),
            f32(F, NX, Q, NY, 128),
            f32(30, 8, 128),
        ),
        in_specs=[VM] * 6,
        out_specs=(VM,) * 3,
        input_output_aliases={5: 0},
        scratch_shapes=[pltpu.VMEM((4, F, Q, 8, 128), jnp.float32)],
        compiler_params=params(),
        cost_estimate=cost(0),
        name="inner",
    )(b, h, own, r0, r1, y)


def halo_image(b, h, y, first, second, s0, x, halo):
    count_x, count_y = lax.axis_size("gx"), lax.axis_size("gy")
    ax, ay = lax.axis_index("gx"), lax.axis_index("gy")
    valid = jnp.where(x == 0, ax > 0, ax < count_x - 1)

    def chunk(r):
        for q in range(Q):
            c = h[x + 1, q, pl.ds(r + TOP, 8), :] + h[halo, q, pl.ds(r + TOP, 8), :]
            for f in range(F):
                a = (f * Q + q) * NY + r
                flux = c * (b[f, x, q, pl.ds(r + TOP, 8), :] - first[pl.ds(a, 8), :])
                other = second[pl.ds(s0 + a, 8), :] - flux
                y[f, halo, q, pl.ds(r + TOP, 8), :] = jnp.where(valid, other, 0.0)

    chunk_loop(chunk)
    for side in range(2):
        row = TOP - 1 if side == 0 else TOP + NY
        valid_row = ay > 0 if side == 0 else ay < count_y - 1
        base = s0 + F * PLANE + side * CORNER
        for q in range(Q):
            h_r = h[x + 1, q, row : row + 1, :]
            a = base + F * Q + q
            c = h_r + inside(second[a : a + 1, :], h_r)
            for f in range(F):
                v = b[f, x, q, row : row + 1, :]
                a = base + f * Q + q
                flux = jnp.where(valid_row, c * (v - second[a : a + 1, :]), 0.0)
                y[f, x + 1, q, row : row + 1, :] = y[f, x + 1, q, row : row + 1, :] + flux


def near_kernel(b, h_in, rin, y_in, z_in, acc_in, h, y, z, acc):
    del h_in, y_in, z_in
    par = lax.axis_index("gx") % 2
    _, near, _, halo = side_planes(par)
    acc[...] = acc_in[...]
    border(b, h, y, rin, near, halo)
    halo_image(b, h, y, rin, rin, L1_ROWS, near, halo)
    plane_grams(b, y, acc, near)

    def z_loop(n, carry):
        z_plane(h, y, z, acc, jnp.where(par == 0, n, NX - 1 - n))
        return carry

    lax.fori_loop(NX - 2, NX, z_loop, 0)


def near_side(b, h, rin, y, z, acc):
    return pl.pallas_call(
        near_kernel,
        out_shape=(
            f32(NX + 2, Q, ROWS, 128),
            f32(F, NX + 2, Q, ROWS, 128),
            f32(F, NX, Q, NY, 128),
            f32(30, 8, 128),
        ),
        in_specs=[VM] * 6,
        out_specs=(VM,) * 4,
        input_output_aliases={1: 0, 3: 1, 4: 2},
        compiler_params=params(),
        cost_estimate=cost(0),
        name="near",
    )(b, h, rin, y, z, acc)


def far_kernel(b, h, rl1, rl2, y_in, z_in, accb, acc_in, y, z, msg, acc):
    del y_in, z_in
    par = lax.axis_index("gx") % 2
    far, _, halo, _ = side_planes(par)
    acc[...] = acc_in[...]
    halo_image(b, h, y, rl1, rl2, 0, far, halo)
    z_plane(h, y, z, acc, far)
    sums = jnp.concatenate(
        [jnp.sum(accb[k], axis=0, keepdims=True) for k in range(10)]
        + [jnp.sum(acc[k], axis=0, keepdims=True) for k in range(30)]
        + [jnp.zeros((88, 128), jnp.float32)],
        axis=0,
    )
    msg[...] = lax.dot_general(
        jnp.ones((8, 128), jnp.float32),
        sums,
        (((1,), (1,)), ((), ())),
        precision=lax.Precision.HIGHEST,
        preferred_element_type=jnp.float32,
    )


def far_side(b, h, rl1, rl2, y, z, accb, acc):
    return pl.pallas_call(
        far_kernel,
        out_shape=(f32(F, NX + 2, Q, ROWS, 128), f32(F, NX, Q, NY, 128), f32(8, 128)),
        in_specs=[VM] * 8,
        out_specs=(VM,) * 3,
        input_output_aliases={4: 0, 5: 1},
        scratch_shapes=[pltpu.VMEM((30, 8, 128), jnp.float32)],
        compiler_params=params(),
        cost_estimate=cost(3),
        name="far",
    )(b, h, rl1, rl2, y, z, accb, acc)


def mm(a, b, ta=False):
    at = (lambda i, k: a[k][i]) if ta else (lambda i, k: a[i][k])
    return [
        [sum((at(i, k) * b[k][j] for k in range(1, F)), at(i, 0) * b[0][j]) for j in range(F)]
        for i in range(F)
    ]


def add(a, b, s=1.0):
    return [[a[i][j] + s * b[i][j] for j in range(F)] for i in range(F)]


def symmetric(a):
    return [[a[i][j] if i == j else 0.5 * (a[i][j] + a[j][i]) for j in range(F)] for i in range(F)]


def spd_solve(a, b):
    low = [[None] * F for _ in range(F)]
    d, inv = [None] * F, [None] * F
    for j in range(F):
        t = a[j][j]
        for k in range(j):
            t = t - low[j][k] * low[j][k] * d[k]
        d[j] = t
        inv[j] = 1.0 / t
        for i in range(j + 1, F):
            t = a[i][j]
            for k in range(j):
                t = t - low[i][k] * low[j][k] * d[k]
            low[i][j] = t * inv[j]
    x = [list(row) for row in b]
    for i in range(F):
        for k in range(i):
            for j in range(F):
                x[i][j] = x[i][j] - low[i][k] * x[k][j]
    for i in range(F):
        x[i] = [e * inv[i] for e in x[i]]
    for i in reversed(range(F)):
        for k in range(i + 1, F):
            for j in range(F):
                x[i][j] = x[i][j] - low[k][i] * x[k][j]
    return x


def step_matrices(entry):
    grams = []
    for g in range(4):
        m = [[None] * F for _ in range(F)]
        for n, (i, j) in enumerate(PAIRS):
            m[i][j] = m[j][i] = entry(10 * g + n)
        grams.append(m)
    bb, by, yy, yd = grams
    yz = add(yd, yy)
    alpha = spd_solve(by, bb)
    new = symmetric(add(mm(alpha, mm(yy, alpha), ta=True), bb, -1.0))
    beta = spd_solve(bb, new)
    e = [[beta[i][j] + 1.0 if i == j else beta[i][j] for j in range(F)] for i in range(F)]
    cross = mm(e, mm(yy, alpha), ta=True)
    curv = add(mm(e, mm(by, e), ta=True), mm(alpha, mm(yz, alpha), ta=True))
    curv = [[curv[i][j] - cross[i][j] - cross[j][i] for j in range(F)] for i in range(F)]
    alpha2 = spd_solve(symmetric(curv), new)
    m1 = add(alpha, mm(e, alpha2))
    m2 = mm(alpha, alpha2)
    return m1, m2


def final_kernel(w, b, y, d, xs_hbm, res_hbm, coef, xs_out, res_out, sems):
    total = jnp.sum(w[...], axis=0, keepdims=True)
    sub = lax.broadcasted_iota(jnp.int32, (128, 128), 0)
    lane = lax.broadcasted_iota(jnp.int32, (128, 128), 1)
    spread = lax.dot_general(
        jnp.where(sub == lane, total, 0.0),
        jnp.ones((128, 128), jnp.float32),
        (((1,), (0,)), ((), ())),
        precision=lax.Precision.HIGHEST,
        preferred_element_type=jnp.float32,
    )
    m1, m2 = step_matrices(lambda k: spread[k : k + 1, :])
    for i in range(F):
        for j in range(F):
            n = i * F + j
            coef[n] = jnp.broadcast_to(m1[i][j], (8, 128))
            coef[16 + n] = jnp.broadcast_to(m2[i][j], (8, 128))
            coef[32 + n] = jnp.broadcast_to(m1[i][j] - m2[i][j], (8, 128))

    def copies(x):
        return (
            pltpu.make_async_copy(xs_out.at[:, x], xs_hbm.at[:, x], sems.at[0, x]),
            pltpu.make_async_copy(res_out.at[:, x], res_hbm.at[:, x], sems.at[1, x]),
        )

    def plane(x, carry):
        def body(i, inner):
            r = pl.multiple_of(i * 8, 8)
            for q in range(Q):
                bs = [b[f, x, q, pl.ds(r + TOP, 8), :] for f in range(F)]
                ys = [y[f, x + 1, q, pl.ds(r + TOP, 8), :] for f in range(F)]
                ds = [d[f, x, q, pl.ds(r, 8), :] for f in range(F)]
                es = [bs[f] - ys[f] for f in range(F)]
                for j in range(F):
                    p = ys[0] * coef[32 + j]
                    for k in range(1, F):
                        p = p + ys[k] * coef[32 + k * F + j]
                    ro = bs[j] - p
                    for k in range(F):
                        p = p + es[k] * coef[k * F + j]
                        ro = ro + ds[k] * coef[16 + k * F + j]
                    s = slice(q * 128, q * 128 + 128)
                    xs_out[j, x, pl.ds(r, 8), s] = p
                    res_out[j, x, pl.ds(r, 8), s] = ro
            return inner

        lax.fori_loop(0, CHUNKS, body, 0)
        for c in copies(x):
            c.start()
        return carry

    lax.fori_loop(0, NX, plane, 0)
    for x in range(NX):
        for c in copies(x):
            c.wait()


def final(w, b, y, d):
    out = jax.ShapeDtypeStruct((F, NX, NY, NZ), jnp.float32)
    return pl.pallas_call(
        final_kernel,
        out_shape=(out, out),
        in_specs=[VM] * 4,
        out_specs=(HBM, HBM),
        scratch_shapes=[
            pltpu.VMEM((48, 8, 128), jnp.float32),
            pltpu.VMEM((F, NX, NY, NZ), jnp.float32),
            pltpu.VMEM((F, NX, NY, NZ), jnp.float32),
            pltpu.SemaphoreType.DMA((2, NX)),
        ],
        compiler_params=params(),
        cost_estimate=cost(5),
        name="final",
    )(w, b, y, d)


def exchange(x, sizes, partner):
    nx, ny = sizes
    pairs = []
    for a in range(nx):
        for c in range(ny):
            ta, tc = partner(a, c)
            if 0 <= ta < nx and 0 <= tc < ny:
                pairs.append((a * ny + c, ta * ny + tc))
    return lax.ppermute(x, AXES, pairs)


def shards(sizes, adjoint_source, conductivity, electrodes):
    nx, ny = sizes
    current = math.sqrt(nx * NX * ny * NY * NZ)
    border_pair = lambda a, c: (a + 1 if a % 2 else a - 1, c)
    inputs = (current, adjoint_source, conductivity, electrodes)
    l1, g0, g1, own = pack(*inputs)
    rl1 = exchange(l1, sizes, border_pair)
    r0 = exchange(g0, sizes, lambda a, c: (a, c ^ 1))
    r1 = exchange(g1, sizes, lambda a, c: (a, c + 1 if c % 2 else c - 1))
    b, h, y, accb = load_fields(*inputs)
    b, h, y, g, l2 = far_edge(b, h, y, own, r0, r1)
    rl2 = exchange(l2, sizes, border_pair)
    h, y, core = near_edge(b, h, y, g, rl1)
    rin = exchange(core, sizes, lambda a, c: (a ^ 1, c))
    y, z, acc = inner(b, h, own, r0, r1, y)
    h, y, z, acc = near_side(b, h, rin, y, z, acc)
    y, z, msg = far_side(b, h, rl1, rl2, y, z, accb, acc)
    sent = jnp.broadcast_to(msg[0:1][None], (nx * ny, 1, 128))
    w = lax.all_to_all(sent, AXES, 0, 0).reshape(nx * ny, 128)
    return final(w, b, y, z)


def solution(mesh):
    sizes = (mesh.shape["gx"], mesh.shape["gy"])
    placed = (P(None, "gx", "gy", None), P("gx", "gy", None), P())
    return jax.shard_map(
        functools.partial(shards, sizes),
        mesh=mesh,
        in_specs=placed,
        out_specs=(P(None, "gx", "gy", None), P(None, "gx", "gy", None)),
        check_vma=False,
    )
```

```python
import functools
import math

import jax
import jax.numpy as jnp
from jax import lax
from jax.experimental import pallas as pl
from jax.experimental.pallas import tpu as pltpu
from jax.sharding import PartitionSpec as P

AXES = ("gx", "gy")
F = 4
NX = 8
NY = 64
NZ = 512
Q = NZ // 128
CHUNKS = NY // 8
UNROLL = 4
PAIRS = [(i, j) for i in range(F) for j in range(i, F)]
TOP = 8
ROWS = NY + 2 * TOP
PLANE = Q * NY
L1_ROWS = (F + 1) * PLANE
CORNER = 24
L2_ROWS = F * PLANE + 2 * CORNER
IN_ROWS = L1_ROWS + L2_ROWS
TILE_ROWS = (F + 1) * Q * 8
G_ROWS = TILE_ROWS + F * Q * 8
VMEM_LIMIT = 16 * 1024 * 1024

VM = pl.BlockSpec(memory_space=pltpu.VMEM)
HBM = pl.BlockSpec(memory_space=pltpu.HBM)


def f32(*shape):
    return pltpu.VMEM(shape, jnp.float32)


def params():
    return pltpu.CompilerParams(vmem_limit_bytes=VMEM_LIMIT)


def cost(us):
    return pl.CostEstimate(flops=int(us * 4e6), bytes_accessed=int(us * 3.0e6), transcendentals=0)


def in_hbm(*arrays):
    return tuple(pltpu.with_memory_space_constraint(a, pltpu.HBM) for a in arrays)


def iota(dim):
    return lax.broadcasted_iota(jnp.int32, (8, 128), dim)


def inside(h_other, h):
    return jnp.where(h_other > 0.0, h_other, h)


def above_z(v):
    t = [pltpu.roll(a, 127, 1) for a in v]
    last = iota(1) == 127
    return [jnp.where(last, t[q + 1], t[q]) if q < Q - 1 else t[q] for q in range(Q)]


def below_z(v):
    t = [pltpu.roll(a, 1, 1) for a in v]
    first = iota(1) == 0
    return [jnp.where(first, t[q - 1], t[q]) if q > 0 else t[q] for q in range(Q)]


def z_coeffs(h):
    up = [a + b for a, b in zip(h, above_z(h))]
    down = [a + b for a, b in zip(h, below_z(h))]
    first, last = iota(1) == 0, iota(1) == 127
    total = [a + b for a, b in zip(up, down)]
    total[0] = up[0] + jnp.where(first, 2.0 * h[0], down[0])
    total[-1] = jnp.where(last, 2.0 * h[-1], up[-1]) + down[-1]
    down[0] = jnp.where(first, 0.0, down[0])
    up[-1] = jnp.where(last, 0.0, up[-1])
    return up, down, total


def add_gram(acc, base, left, right):
    for n, (i, j) in enumerate(PAIRS):
        t = left[i][0] * right[j][0]
        for q in range(1, Q):
            t = t + left[i][q] * right[j][q]
        acc[base + n] += t


def chunk_loop(body):
    def step(i, carry):
        for u in range(UNROLL):
            body(pl.multiple_of(i * (8 * UNROLL), 8) + 8 * u)
        return carry

    lax.fori_loop(0, CHUNKS // UNROLL, step, 0)


def tiles_of(ref, index, row):
    return [ref[(*index, q, pl.ds(row, 8), slice(None))] for q in range(Q)]


def add_spike(ref, index, row, current):
    tile = ref[(*index, slice(0, 128))]
    ref[(*index, slice(0, 128))] = tile + jnp.where(
        (iota(0) == row) & (iota(1) == 0), current, 0.0
    )


def local_cell(elec, f):
    total_y = NY * lax.axis_size("gy")
    cell = elec[f]
    lx = cell // total_y - lax.axis_index("gx") * NX
    ly = cell % total_y - lax.axis_index("gy") * NY
    return lx, ly, (lx >= 0) & (lx < NX) & (ly >= 0) & (ly < NY)


def pack_kernel(
    current, adj, sigma, elec_in, l1_out, g0_out, g1_out, own_out, plane, tiles, far_rows, elec, sems, esem
):
    par = lax.axis_index("gx") % 2
    ypar = lax.axis_index("gy") % 2
    edge = par * (NX - 1)
    ecopy = pltpu.make_async_copy(elec_in, elec, esem)
    ecopy.start()
    copies = []
    for f in range(F + 1):
        src = adj.at[f] if f < F else sigma
        copies.append(pltpu.make_async_copy(src.at[edge], plane.at[f], sems.at[0, f]))
        for side, y in ((0, 0), (1, NY - 8)):
            copies.append(
                pltpu.make_async_copy(
                    src.at[:, pl.ds(y, 8), :], tiles.at[f, side], sems.at[1 + side, f]
                )
            )
    for c in copies:
        c.start()
    ecopy.wait()
    for c in copies:
        c.wait()
    for f in range(F):
        lx, ly, here = local_cell(elec, f)

        @pl.when(here & (lx == edge))
        def _(f=f, ly=ly):
            r8 = pl.multiple_of((ly // 8) * 8, 8)
            add_spike(plane, (f, pl.ds(r8, 8)), ly - r8, current)

        @pl.when(here & (ly < 8))
        def _(f=f, lx=lx, ly=ly):
            add_spike(tiles, (f, 0, lx, slice(0, 8)), ly, current)

        @pl.when(here & (ly >= NY - 8))
        def _(f=f, lx=lx, ly=ly):
            add_spike(tiles, (f, 1, lx, slice(0, 8)), ly - (NY - 8), current)

    for f in range(F + 1):
        k = 1.0 if f < F else 0.5
        for q in range(Q):
            s = slice(q * 128, q * 128 + 128)
            a = (f * Q + q) * NY
            l1_out[a : a + NY, :] = k * plane[f, :, s]
            for x in range(NX):
                a = (f * Q + q) * 8 + x
                for side, (near, far) in enumerate(((0, 1), (7, 6))):
                    own_out[side, a : a + 1, :] = k * tiles[f, side, x, near : near + 1, s]
                    far_rows[side, a : a + 1, :] = k * tiles[f, side, x, far : far + 1, s]
    for f in range(F + 1):
        for q in range(Q):
            t = slice((f * Q + q) * 8, (f * Q + q) * 8 + 8)
            lo, hi = own_out[0, t, :], own_out[1, t, :]
            g0_out[t, :] = jnp.where(ypar == 0, hi, lo)
            g1_out[t, :] = jnp.where(ypar == 0, lo, hi)
            if f < F:
                ht = slice((F * Q + q) * 8, (F * Q + q) * 8 + 8)
                lo = (own_out[0, ht, :] + far_rows[0, ht, :]) * (lo - far_rows[0, t, :])
                hi = (own_out[1, ht, :] + far_rows[1, ht, :]) * (hi - far_rows[1, t, :])
                d = slice(TILE_ROWS + (f * Q + q) * 8, TILE_ROWS + (f * Q + q) * 8 + 8)
                g0_out[d, :] = jnp.where(ypar == 0, hi, lo)
                g1_out[d, :] = jnp.where(ypar == 0, lo, hi)


def pack(current, adj, sigma, electrodes):
    return pl.pallas_call(
        functools.partial(pack_kernel, current),
        out_shape=(
            f32(L1_ROWS, 128),
            f32(G_ROWS, 128),
            f32(G_ROWS, 128),
            f32(2, TILE_ROWS, 128),
        ),
        in_specs=[HBM] * 3,
        out_specs=(VM,) * 4,
        scratch_shapes=[
            pltpu.VMEM((F + 1, NY, NZ), jnp.float32),
            pltpu.VMEM((F + 1, 2, NX, 8, NZ), jnp.float32),
            pltpu.VMEM((2, TILE_ROWS, 128), jnp.float32),
            pltpu.SMEM((F,), jnp.int32),
            pltpu.SemaphoreType.DMA((3, F + 1)),
            pltpu.SemaphoreType.DMA,
        ],
        compiler_params=params(),
        cost_estimate=cost(2),
        name="pack",
    )(*in_hbm(adj, sigma, electrodes))


def load_kernel(current, adj, sigma, elec_in, b_out, h_out, y, acc, elec, esem):
    ecopy = pltpu.make_async_copy(elec_in, elec, esem)
    ecopy.start()
    acc[...] = jnp.zeros(acc.shape, jnp.float32)

    def place(x, carry):
        for q in range(Q):
            s = slice(q * 128, q * 128 + 128)
            for f in range(F):
                b_out[f, x, q, TOP : TOP + NY, :] = adj[f, x, :, s]
            h_out[x + 1, q, TOP : TOP + NY, :] = 0.5 * sigma[x, :, s]
            for row, edge in ((TOP - 1, TOP), (TOP + NY, TOP + NY - 1)):
                h_out[x + 1, q, row : row + 1, :] = -h_out[x + 1, q, edge : edge + 1, :]
                for f in range(F):
                    b_out[f, x, q, row : row + 1, :] = jnp.zeros((1, 128), jnp.float32)
        return carry

    lax.fori_loop(0, NX, place, 0)
    ecopy.wait()
    for f in range(F):
        lx, ly, here = local_cell(elec, f)

        @pl.when(here)
        def _(f=f, lx=lx, ly=ly):
            r8 = pl.multiple_of((ly // 8) * 8, 8)
            add_spike(b_out, (f, lx, 0, pl.ds(r8 + TOP, 8)), ly - r8, current)

    def plane(x, carry):
        def chunk(r):
            vs = [tiles_of(b_out, (f, x), r + TOP) for f in range(F)]
            add_gram(acc, 0, vs, vs)

        chunk_loop(chunk)
        return carry

    lax.fori_loop(0, NX, plane, 0)

    def image(x, carry):
        def chunk(r):
            coeffs = chunk_coeffs(h_out, x + 1, r)
            for f in range(F):
                _, out = chunk_apply(coeffs, b_out, f, x, r)
                for q in range(Q):
                    y[f, x + 1, q, pl.ds(r + TOP, 8), :] = out[q]

        chunk_loop(chunk)
        return carry

    lax.fori_loop(1, NX - 1, image, 0)


def load_fields(current, adj, sigma, electrodes):
    return pl.pallas_call(
        functools.partial(load_kernel, current),
        out_shape=(
            f32(F, NX, Q, ROWS, 128),
            f32(NX + 2, Q, ROWS, 128),
            f32(F, NX + 2, Q, ROWS, 128),
            f32(10, 8, 128),
        ),
        in_specs=[VM, VM, HBM],
        out_specs=(VM,) * 4,
        scratch_shapes=[pltpu.SMEM((F,), jnp.int32), pltpu.SemaphoreType.DMA],
        compiler_params=params(),
        cost_estimate=cost(2),
        name="load",
    )(adj, sigma, *in_hbm(electrodes))


def chunk_coeffs(h, k, r, x_steps=(-1, 1)):
    at = r + TOP
    own = tiles_of(h, (k,), at)
    up, down, total = z_coeffs(own)
    faces = [(None, up), (None, down)]
    others = [((0, 1), tiles_of(h, (k,), at + 1)), ((0, -1), tiles_of(h, (k,), at - 1))]
    others += [((s, 0), tiles_of(h, (k + s,), at)) for s in x_steps]
    for step, other in others:
        c = [a + b for a, b in zip(own, other)]
        total = [a + b for a, b in zip(total, c)]
        faces.append((step, c))
    return total, faces


def chunk_apply(coeffs, v, f, k, r):
    total, faces = coeffs
    at = r + TOP
    own = tiles_of(v, (f, k), at)
    out = []
    up, down = above_z(own), below_z(own)
    for q in range(Q):
        t = total[q] * own[q] - faces[0][1][q] * up[q] - faces[1][1][q] * down[q]
        u = None
        for s, c in faces[2:]:
            n = c[q] * v[f, k + s[0], q, pl.ds(at + s[1], 8), :]
            u = n if u is None else u + n
        out.append(t - u)
    return own, out


def side_planes(par):
    far = par * (NX - 1)
    near = (NX - 1) - far
    return far, near, par * (NX + 1), (1 - par) * (NX + 1)


def halo_select(ypar, r0, r1, item):
    a = r0[item * 8 : item * 8 + 8, :]
    b = r1[item * 8 : item * 8 + 8, :]
    return jnp.where(ypar == 0, b, a), jnp.where(ypar == 0, a, b)


def edge_plane(b, h, y, x, step):
    def chunk(r):
        coeffs = chunk_coeffs(h, x + 1, r, (step,))
        for f in range(F):
            _, out = chunk_apply(coeffs, b, f, x, r)
            for q in range(Q):
                y[f, x + 1, q, pl.ds(r + TOP, 8), :] = out[q]

    chunk_loop(chunk)


def put_image(y, g, out, base, x):
    for item in range(F * Q):
        f, q = divmod(item, Q)
        a = base + item * NY
        out[a : a + NY, :] = y[f, x + 1, q, TOP : TOP + NY, :]
    base = base + F * PLANE
    out[base : base + 2 * CORNER, :] = jnp.zeros((2 * CORNER, 128), jnp.float32)
    for side in range(2):
        for item in range((F + 1) * Q):
            a = base + side * CORNER + item
            out[a : a + 1, :] = g[side, pl.ds(item * 8 + x, 1), :]


def far_edge_kernel(b_in, h_in, y_in, own, r0, r1, b, h, y, out, core, g, clamped):
    del b_in, h_in, y_in
    par = lax.axis_index("gx") % 2
    ypar = lax.axis_index("gy") % 2
    for item in range((F + 1) * Q):
        f, q = divmod(item, Q)
        for side, t in enumerate(halo_select(ypar, r0, r1, item)):
            row = TOP - 1 if side == 0 else TOP + NY
            g[side, item * 8 : item * 8 + 8, :] = t
            if f < F:
                for x in range(NX):
                    b[f, x, q, row : row + 1, :] = g[side, item * 8 + x : item * 8 + x + 1, :]
            else:
                clamped[side, q] = inside(t, own[side, item * 8 : item * 8 + 8, :])
                for x in range(NX):
                    h[x + 1, q, row : row + 1, :] = clamped[side, q, x : x + 1, :]
    far, near, _, _ = side_planes(par)
    edge_plane(b, h, y, far, 1 - 2 * par)
    put_image(y, g, out, 0, far)
    edge_plane(b, h, y, near, 2 * par - 1)
    for q in range(Q):
        for f in range(F):
            a = (f * Q + q) * NY
            core[a : a + NY, :] = b[f, near, q, TOP : TOP + NY, :]
        a = (F * Q + q) * NY
        core[a : a + NY, :] = h[near + 1, q, TOP : TOP + NY, :]
    put_image(y, g, core, L1_ROWS, near)


def border_kernel(b, h_in, y_in, core_in, rl1, h, y, core):
    del h_in, y_in, core_in, core
    par = lax.axis_index("gx") % 2
    far, _, far_halo, _ = side_planes(par)
    border(b, h, y, rl1, far, far_halo)


def border(b, h, y, first, x, halo):
    def chunk(r):
        for q in range(Q):
            own = h[x + 1, q, pl.ds(r + TOP, 8), :]
            beyond = inside(first[pl.ds((F * Q + q) * NY + r, 8), :], own)
            h[halo, q, pl.ds(r + TOP, 8), :] = beyond
            c = own + beyond
            for f in range(F):
                v = b[f, x, q, pl.ds(r + TOP, 8), :]
                flux = c * (v - first[pl.ds((f * Q + q) * NY + r, 8), :])
                at = (f, x + 1, q, pl.ds(r + TOP, 8), slice(None))
                y[at] = y[at] + flux

    chunk_loop(chunk)


def far_edge(b, h, y, own, r0, r1):
    return pl.pallas_call(
        far_edge_kernel,
        out_shape=(
            f32(F, NX, Q, ROWS, 128),
            f32(NX + 2, Q, ROWS, 128),
            f32(F, NX + 2, Q, ROWS, 128),
            f32(L2_ROWS, 128),
            f32(IN_ROWS, 128),
        ),
        in_specs=[VM] * 6,
        out_specs=(VM,) * 5,
        input_output_aliases={0: 0, 1: 1, 2: 2},
        scratch_shapes=[
            pltpu.VMEM((2, TILE_ROWS, 128), jnp.float32),
            pltpu.VMEM((2, Q, 8, 128), jnp.float32),
        ],
        compiler_params=params(),
        cost_estimate=cost(10),
        name="far_edge",
    )(b, h, y, own, r0, r1)


def border_faces(b, h, y, core, rl1):
    return pl.pallas_call(
        border_kernel,
        out_shape=(f32(NX + 2, Q, ROWS, 128), f32(F, NX + 2, Q, ROWS, 128), f32(IN_ROWS, 128)),
        in_specs=[VM] * 5,
        out_specs=(VM,) * 3,
        input_output_aliases={1: 0, 2: 1, 3: 2},
        compiler_params=params(),
        cost_estimate=cost(20),
        name="border",
    )(b, h, y, core, rl1)


def row_halo(own, rh, side, y, tmp):
    count = lax.axis_size("gy")
    ay = lax.axis_index("gy")
    valid = ay > 0 if side == 0 else ay < count - 1
    row = TOP - 1 if side == 0 else TOP + NY
    sub = iota(0)
    own_at = lambda f, q: own[side, (f * Q + q) * 8 : (f * Q + q) * 8 + 8, :]
    h_r = [rh(F * Q + q) for q in range(Q)]
    zu, zd, total = z_coeffs(h_r)
    across = [h_r[q] + own_at(F, q) for q in range(Q)]
    up = [jnp.where(sub == NX - 1, 0.0, a + pltpu.roll(a, 7, 0)) for a in h_r]
    down = [jnp.where(sub == 0, 0.0, a + pltpu.roll(a, 1, 0)) for a in h_r]
    total = [sum(t) for t in zip(total, across, up, down)]
    for f in range(F):
        v = [rh(f * Q + q) for q in range(Q)]
        zp, zm = above_z(v), below_z(v)
        for q in range(Q):
            out = total[q] * v[q] + rh((F + 1 + f) * Q + q) - across[q] * own_at(f, q)
            out = out - up[q] * pltpu.roll(v[q], 7, 0) - down[q] * pltpu.roll(v[q], 1, 0)
            out = out - zu[q] * zp[q] - zd[q] * zm[q]
            tmp[side, f, q] = jnp.where(valid, out, 0.0)
            for x in range(NX):
                y[f, x + 1, q, row : row + 1, :] = tmp[side, f, q, x : x + 1, :]


def halo_rows(own, rh, y, tmp):
    for side in range(2):
        row = TOP if side == 0 else TOP + NY - 1
        for q in range(Q):
            h_own = own[side, (F * Q + q) * 8 : (F * Q + q) * 8 + 8, :]
            c = h_own + inside(rh(F * Q + q)[side], h_own)
            for f in range(F):
                item = f * Q + q
                tmp[2 + side, f, q] = c * (own[side, item * 8 : item * 8 + 8, :] - rh(item)[side])
                for x in range(1, NX - 1):
                    y[f, x + 1, q, row : row + 1, :] += tmp[2 + side, f, q, x : x + 1, :]


def z_plane(h, y, d, acc, x):
    def chunk(r):
        coeffs = chunk_coeffs(h, x + 1, r)
        for f in range(F):
            v, out = chunk_apply(coeffs, y, f, x + 1, r)
            for q in range(Q):
                d[f, x, q, pl.ds(r, 8), :] = out[q] - v[q]

    def grams(r):
        ys = [tiles_of(y, (f, x + 1), r + TOP) for f in range(F)]
        add_gram(acc, 20, ys, [tiles_of(d, (f, x), r) for f in range(F)])

    chunk_loop(chunk)
    chunk_loop(grams)


def plane_grams(b, y, acc, x):
    def chunk(r):
        vs = [tiles_of(b, (f, x), r + TOP) for f in range(F)]
        outs = [tiles_of(y, (f, x + 1), r + TOP) for f in range(F)]
        add_gram(acc, 0, vs, outs)
        add_gram(acc, 10, outs, outs)

    chunk_loop(chunk)


def inner_kernel(b, h, own, r0, r1, y_in, y, z, acc, tmp):
    del y_in
    par = lax.axis_index("gx") % 2
    ypar = lax.axis_index("gy") % 2
    far = side_planes(par)[0]
    acc[...] = jnp.zeros(acc.shape, jnp.float32)
    for side in range(2):
        row_halo(own, lambda item: halo_select(ypar, r0, r1, item)[side], side, y, tmp)

    halo_rows(own, lambda item: halo_select(ypar, r0, r1, item), y, tmp)

    def y_plane(x, carry):
        plane_grams(b, y, acc, x)
        return carry

    lax.fori_loop(1, NX - 1, y_plane, 0)
    plane_grams(b, y, acc, far)

    def z_loop(n, carry):
        z_plane(h, y, z, acc, jnp.where(par == 0, n, NX - 1 - n))
        return carry

    lax.fori_loop(1, NX - 2, z_loop, 0)


def inner(b, h, own, r0, r1, y):
    return pl.pallas_call(
        inner_kernel,
        out_shape=(
            f32(F, NX + 2, Q, ROWS, 128),
            f32(F, NX, Q, NY, 128),
            f32(30, 8, 128),
        ),
        in_specs=[VM] * 6,
        out_specs=(VM,) * 3,
        input_output_aliases={5: 0},
        scratch_shapes=[pltpu.VMEM((4, F, Q, 8, 128), jnp.float32)],
        compiler_params=params(),
        cost_estimate=cost(0),
        name="inner",
    )(b, h, own, r0, r1, y)


def halo_image(b, h, y, first, second, s0, x, halo):
    count_x, count_y = lax.axis_size("gx"), lax.axis_size("gy")
    ax, ay = lax.axis_index("gx"), lax.axis_index("gy")
    valid = jnp.where(x == 0, ax > 0, ax < count_x - 1)

    def chunk(r):
        for q in range(Q):
            c = h[x + 1, q, pl.ds(r + TOP, 8), :] + h[halo, q, pl.ds(r + TOP, 8), :]
            for f in range(F):
                a = (f * Q + q) * NY + r
                flux = c * (b[f, x, q, pl.ds(r + TOP, 8), :] - first[pl.ds(a, 8), :])
                other = second[pl.ds(s0 + a, 8), :] - flux
                y[f, halo, q, pl.ds(r + TOP, 8), :] = jnp.where(valid, other, 0.0)

    chunk_loop(chunk)
    for side in range(2):
        row = TOP - 1 if side == 0 else TOP + NY
        valid_row = ay > 0 if side == 0 else ay < count_y - 1
        base = s0 + F * PLANE + side * CORNER
        for q in range(Q):
            h_r = h[x + 1, q, row : row + 1, :]
            a = base + F * Q + q
            c = h_r + inside(second[a : a + 1, :], h_r)
            for f in range(F):
                v = b[f, x, q, row : row + 1, :]
                a = base + f * Q + q
                flux = jnp.where(valid_row, c * (v - second[a : a + 1, :]), 0.0)
                y[f, x + 1, q, row : row + 1, :] = y[f, x + 1, q, row : row + 1, :] + flux


def near_kernel(b, h_in, rin, y_in, z_in, acc_in, h, y, z, acc):
    del h_in, y_in, z_in
    par = lax.axis_index("gx") % 2
    _, near, _, halo = side_planes(par)
    acc[...] = acc_in[...]
    border(b, h, y, rin, near, halo)
    halo_image(b, h, y, rin, rin, L1_ROWS, near, halo)
    plane_grams(b, y, acc, near)

    def z_loop(n, carry):
        z_plane(h, y, z, acc, jnp.where(par == 0, n, NX - 1 - n))
        return carry

    lax.fori_loop(NX - 2, NX, z_loop, 0)


def near_side(b, h, rin, y, z, acc):
    return pl.pallas_call(
        near_kernel,
        out_shape=(
            f32(NX + 2, Q, ROWS, 128),
            f32(F, NX + 2, Q, ROWS, 128),
            f32(F, NX, Q, NY, 128),
            f32(30, 8, 128),
        ),
        in_specs=[VM] * 6,
        out_specs=(VM,) * 4,
        input_output_aliases={1: 0, 3: 1, 4: 2},
        compiler_params=params(),
        cost_estimate=cost(0),
        name="near",
    )(b, h, rin, y, z, acc)


def far_kernel(b, h, rl1, rl2, y_in, z_in, accb, acc_in, y, z, msg, acc):
    del y_in, z_in
    par = lax.axis_index("gx") % 2
    far, _, halo, _ = side_planes(par)
    acc[...] = acc_in[...]
    halo_image(b, h, y, rl1, rl2, 0, far, halo)
    z_plane(h, y, z, acc, far)
    sums = jnp.concatenate(
        [jnp.sum(accb[k], axis=0, keepdims=True) for k in range(10)]
        + [jnp.sum(acc[k], axis=0, keepdims=True) for k in range(30)]
        + [jnp.zeros((88, 128), jnp.float32)],
        axis=0,
    )
    msg[...] = lax.dot_general(
        jnp.ones((8, 128), jnp.float32),
        sums,
        (((1,), (1,)), ((), ())),
        precision=lax.Precision.HIGHEST,
        preferred_element_type=jnp.float32,
    )


def far_side(b, h, rl1, rl2, y, z, accb, acc):
    return pl.pallas_call(
        far_kernel,
        out_shape=(f32(F, NX + 2, Q, ROWS, 128), f32(F, NX, Q, NY, 128), f32(8, 128)),
        in_specs=[VM] * 8,
        out_specs=(VM,) * 3,
        input_output_aliases={4: 0, 5: 1},
        scratch_shapes=[pltpu.VMEM((30, 8, 128), jnp.float32)],
        compiler_params=params(),
        cost_estimate=cost(3),
        name="far",
    )(b, h, rl1, rl2, y, z, accb, acc)


def mm(a, b, ta=False):
    at = (lambda i, k: a[k][i]) if ta else (lambda i, k: a[i][k])
    return [
        [sum((at(i, k) * b[k][j] for k in range(1, F)), at(i, 0) * b[0][j]) for j in range(F)]
        for i in range(F)
    ]


def add(a, b, s=1.0):
    return [[a[i][j] + s * b[i][j] for j in range(F)] for i in range(F)]


def symmetric(a):
    return [[a[i][j] if i == j else 0.5 * (a[i][j] + a[j][i]) for j in range(F)] for i in range(F)]


def spd_solve(a, b):
    low = [[None] * F for _ in range(F)]
    d, inv = [None] * F, [None] * F
    for j in range(F):
        t = a[j][j]
        for k in range(j):
            t = t - low[j][k] * low[j][k] * d[k]
        d[j] = t
        inv[j] = 1.0 / t
        for i in range(j + 1, F):
            t = a[i][j]
            for k in range(j):
                t = t - low[i][k] * low[j][k] * d[k]
            low[i][j] = t * inv[j]
    x = [list(row) for row in b]
    for i in range(F):
        for k in range(i):
            for j in range(F):
                x[i][j] = x[i][j] - low[i][k] * x[k][j]
    for i in range(F):
        x[i] = [e * inv[i] for e in x[i]]
    for i in reversed(range(F)):
        for k in range(i + 1, F):
            for j in range(F):
                x[i][j] = x[i][j] - low[k][i] * x[k][j]
    return x


def step_matrices(entry):
    grams = []
    for g in range(4):
        m = [[None] * F for _ in range(F)]
        for n, (i, j) in enumerate(PAIRS):
            m[i][j] = m[j][i] = entry(10 * g + n)
        grams.append(m)
    bb, by, yy, yd = grams
    yz = add(yd, yy)
    alpha = spd_solve(by, bb)
    new = symmetric(add(mm(alpha, mm(yy, alpha), ta=True), bb, -1.0))
    beta = spd_solve(bb, new)
    e = [[beta[i][j] + 1.0 if i == j else beta[i][j] for j in range(F)] for i in range(F)]
    cross = mm(e, mm(yy, alpha), ta=True)
    curv = add(mm(e, mm(by, e), ta=True), mm(alpha, mm(yz, alpha), ta=True))
    curv = [[curv[i][j] - cross[i][j] - cross[j][i] for j in range(F)] for i in range(F)]
    alpha2 = spd_solve(symmetric(curv), new)
    m1 = add(alpha, mm(e, alpha2))
    m2 = mm(alpha, alpha2)
    return m1, m2


def final_kernel(w, b, y, d, xs_hbm, res_hbm, coef, xs_out, res_out, sems):
    total = jnp.sum(w[...], axis=0, keepdims=True)
    sub = lax.broadcasted_iota(jnp.int32, (128, 128), 0)
    lane = lax.broadcasted_iota(jnp.int32, (128, 128), 1)
    spread = lax.dot_general(
        jnp.where(sub == lane, total, 0.0),
        jnp.ones((128, 128), jnp.float32),
        (((1,), (0,)), ((), ())),
        precision=lax.Precision.HIGHEST,
        preferred_element_type=jnp.float32,
    )
    m1, m2 = step_matrices(lambda k: spread[k : k + 1, :])
    for i in range(F):
        for j in range(F):
            n = i * F + j
            coef[n] = jnp.broadcast_to(m1[i][j], (8, 128))
            coef[16 + n] = jnp.broadcast_to(m2[i][j], (8, 128))
            coef[32 + n] = jnp.broadcast_to(m1[i][j] - m2[i][j], (8, 128))

    def copies(x):
        return (
            pltpu.make_async_copy(xs_out.at[:, x], xs_hbm.at[:, x], sems.at[0, x]),
            pltpu.make_async_copy(res_out.at[:, x], res_hbm.at[:, x], sems.at[1, x]),
        )

    def plane(x, carry):
        def body(i, inner):
            r = pl.multiple_of(i * 8, 8)
            for q in range(Q):
                bs = [b[f, x, q, pl.ds(r + TOP, 8), :] for f in range(F)]
                ys = [y[f, x + 1, q, pl.ds(r + TOP, 8), :] for f in range(F)]
                ds = [d[f, x, q, pl.ds(r, 8), :] for f in range(F)]
                es = [bs[f] - ys[f] for f in range(F)]
                for j in range(F):
                    p = ys[0] * coef[32 + j]
                    for k in range(1, F):
                        p = p + ys[k] * coef[32 + k * F + j]
                    ro = bs[j] - p
                    for k in range(F):
                        p = p + es[k] * coef[k * F + j]
                        ro = ro + ds[k] * coef[16 + k * F + j]
                    s = slice(q * 128, q * 128 + 128)
                    xs_out[j, x, pl.ds(r, 8), s] = p
                    res_out[j, x, pl.ds(r, 8), s] = ro
            return inner

        lax.fori_loop(0, CHUNKS, body, 0)
        for c in copies(x):
            c.start()
        return carry

    lax.fori_loop(0, NX, plane, 0)
    for x in range(NX):
        for c in copies(x):
            c.wait()


def final(w, b, y, d):
    out = jax.ShapeDtypeStruct((F, NX, NY, NZ), jnp.float32)
    return pl.pallas_call(
        final_kernel,
        out_shape=(out, out),
        in_specs=[VM] * 4,
        out_specs=(HBM, HBM),
        scratch_shapes=[
            pltpu.VMEM((48, 8, 128), jnp.float32),
            pltpu.VMEM((F, NX, NY, NZ), jnp.float32),
            pltpu.VMEM((F, NX, NY, NZ), jnp.float32),
            pltpu.SemaphoreType.DMA((2, NX)),
        ],
        compiler_params=params(),
        cost_estimate=cost(5),
        name="final",
    )(w, b, y, d)


def exchange(x, sizes, partner):
    nx, ny = sizes
    pairs = []
    for a in range(nx):
        for c in range(ny):
            ta, tc = partner(a, c)
            if 0 <= ta < nx and 0 <= tc < ny:
                pairs.append((a * ny + c, ta * ny + tc))
    return lax.ppermute(x, AXES, pairs)


def shards(sizes, adjoint_source, conductivity, electrodes):
    nx, ny = sizes
    current = math.sqrt(nx * NX * ny * NY * NZ)
    border_pair = lambda a, c: (a + 1 if a % 2 else a - 1, c)
    inputs = (current, adjoint_source, conductivity, electrodes)
    l1, g0, g1, own = pack(*inputs)
    rl1 = exchange(l1, sizes, border_pair)
    r0 = exchange(g0, sizes, lambda a, c: (a, c ^ 1))
    r1 = exchange(g1, sizes, lambda a, c: (a, c + 1 if c % 2 else c - 1))
    b, h, y, accb = load_fields(*inputs)
    b, h, y, l2, core = far_edge(b, h, y, own, r0, r1)
    rl2 = exchange(l2, sizes, border_pair)
    h, y, core = border_faces(b, h, y, core, rl1)
    rin = exchange(core, sizes, lambda a, c: (a ^ 1, c))
    y, z, acc = inner(b, h, own, r0, r1, y)
    h, y, z, acc = near_side(b, h, rin, y, z, acc)
    y, z, msg = far_side(b, h, rl1, rl2, y, z, accb, acc)
    sent = jnp.broadcast_to(msg[0:1][None], (nx * ny, 1, 128))
    w = lax.all_to_all(sent, AXES, 0, 0).reshape(nx * ny, 128)
    return final(w, b, y, z)


def solution(mesh):
    sizes = (mesh.shape["gx"], mesh.shape["gy"])
    placed = (P(None, "gx", "gy", None), P("gx", "gy", None), P())
    return jax.shard_map(
        functools.partial(shards, sizes),
        mesh=mesh,
        in_specs=placed,
        out_specs=(P(None, "gx", "gy", None), P(None, "gx", "gy", None)),
        check_vma=False,
    )
```
